256 devices in a mesh: bx: 8 (over y_lo, x), by: 8 (over z), bz: 4 (over y_hi, core).
Axes of the slice: x: 4, y: 4 (y_hi: 2, y_lo: 2; y = y_hi * 2 + y_lo), z: 8, core: 2. Of those that a mesh axis runs over, the one named last changes fastest.
Arguments:
- estimate: float32 [128, 128, 512], P('bx', 'by', 'bz'), may hold values from 0.5 to 2
- raw_views: float32 [6, 128, 128, 512], P(None, 'bx', 'by', 'bz'), may hold values from 0.25 to 4
- psf: float32 [6, 3, 31], replicated, may hold values from 0.05 to 1
- offsets: int32 [6, 3], replicated, may hold values from -8 to 8, as said below
- coverage: int32 [6, 8, 8, 4], P(None, 'bx', 'by', 'bz'), may hold values from 0 to 1, as said below
Outputs:
- restored: float32 [128, 128, 512], P('bx', 'by', 'bz')
The draws below stay inside these ranges and needn't reach their ends.
Inputs may be any that keep to these rules, and one draw needn't show every extreme that they name: `offsets`: one view has first component exactly 8 and the next view (cyclically) third component exactly -8. `coverage`: every output block is covered by at least one view.
All inputs are finite; a program needn't handle non-finite values.
Results may differ from the reference program's by a relative error of at most 0.0001.
Values sent between devices are 32-bit elements; how exact they have to be, the bound alone decides.
No kernel may reach another device: no remote copies, remote signals or barrier semaphores. Data moves between devices by JAX's collectives and lax.ppermute only.
A program may use at most 128 MiB of HBM per device.

```python
import math
import jax
import jax.numpy as jnp
from jax import lax

V = 6
K = 31
R = 15
OFF = 8
ITERS = 1
CX = 16
CY = 16
CZ = 128
NX = 128
NY = 128
NZ = 512
N_BX = 8
N_BY = 8
N_BZ = 4


def draw_offsets(key, part):
    key = jax.random.fold_in(key, 11)
    first, second = jax.random.split(key, 2)
    values = jax.random.randint(first, (V, 3), -OFF, OFF + 1)
    chosen = jax.random.randint(second, (), 0, V)
    values = values.at[chosen, 0].set(OFF)
    values = values.at[(chosen + 1) % V, 2].set(-OFF)
    return values.astype(jnp.int32)


def draw_coverage(key, part):
    key = jax.random.fold_in(key, 23)
    first, second = jax.random.split(key, 2)
    base = jax.random.randint(first, (V, N_BX, N_BY, N_BZ), 0, 2)
    chosen = jax.random.randint(second, (N_BX, N_BY, N_BZ), 0, V)
    forced = (jnp.arange(V, dtype=jnp.int32)[:, None, None, None] == chosen[None]).astype(jnp.int32)
    return jnp.maximum(base, forced).astype(jnp.int32)


def levels(key, dims, cuts, low, largest):
    loudness = 1.0
    for dim, blocks in cuts:
        steps = jax.random.uniform(jax.random.fold_in(jax.random.fold_in(key, 6), dim), (blocks,), jnp.float32, low / len(cuts), largest / len(cuts))
        loudness = loudness * jnp.repeat(jnp.exp(steps), dims[dim] // blocks).reshape((-1,) + (1,) * (len(dims) - 1 - dim))
    return loudness


def setup_inputs(seed: int = 0) -> dict:
    keys = jax.random.split(jax.random.key(seed), 6)
    estimate = jnp.clip(jnp.exp(math.log(2.0) - 1.3862944 * jax.random.uniform(keys[0], (NX, NY, NZ), jnp.float32) ** levels(keys[0], (NX, NY, NZ), ((0, 8), (1, 8), (2, 4)), -0.2, 0.2)), 0.5, 2.0)
    raw_views = jnp.clip(jnp.exp(math.log(4.0) - 2.7725887 * jax.random.uniform(keys[1], (V, NX, NY, NZ), jnp.float32) ** levels(keys[1], (V, NX, NY, NZ), ((1, 8), (2, 8), (3, 4)), -0.2, 0.2)), 0.25, 4.0)
    psf = jnp.clip(jnp.exp(jax.random.uniform(keys[2], (V, 3, K), jnp.float32, math.log(0.05), math.log(1.0))), 0.05, 1.0)
    offsets = draw_offsets(jax.random.fold_in(keys[5], 71), 0)
    coverage = draw_coverage(jax.random.fold_in(keys[5], 71), 0)
    return dict(estimate=estimate, raw_views=raw_views, psf=psf, offsets=offsets, coverage=coverage)


def along_axis(field, kernel, axis):
    moved = jnp.moveaxis(field, axis, -1)
    shape = moved.shape
    flat = moved.reshape(-1, 1, shape[-1])
    result = lax.conv_general_dilated(flat, kernel.reshape(1, 1, -1), (1,), [(R, R)], precision=lax.Precision.HIGHEST)
    return jnp.moveaxis(result.reshape(shape), -1, axis)


def blur(field, kernels, flipped):
    for axis in range(3):
        kernel = kernels[axis]
        if flipped:
            kernel = jnp.flip(kernel)
        field = along_axis(field, kernel, axis)
    return field


def reference(estimate, raw_views, psf, offsets, coverage):
    kernels = psf / jnp.sum(psf, axis=2, keepdims=True)
    observed = []
    masks = []
    weights = jnp.zeros((NX, NY, NZ), jnp.float32)
    for view in range(V):
        padded = jnp.pad(raw_views[view], OFF)
        starts = (OFF + offsets[view, 0], OFF + offsets[view, 1], OFF + offsets[view, 2])
        observed.append(lax.dynamic_slice(padded, starts, (NX, NY, NZ)))
        blocks = coverage[view].astype(jnp.float32)[:, None, :, None, :, None]
        mask = jnp.broadcast_to(blocks, (N_BX, CX, N_BY, CY, N_BZ, CZ)).reshape(NX, NY, NZ)
        masks.append(mask)
        weights = weights + blur(mask, kernels[view], True)
    restored = estimate
    for step in range(ITERS):
        total = jnp.zeros((NX, NY, NZ), jnp.float32)
        for view in range(V):
            ratio = masks[view] * observed[view] / blur(restored, kernels[view], False)
            total = total + blur(ratio, kernels[view], True)
        restored = restored * total / weights
    return restored
```

```python
import jax
import jax.numpy as jnp
from jax import lax
from jax.experimental import pallas as pl
from jax.experimental.pallas import tpu as pltpu
from jax.sharding import PartitionSpec as P

V = 6
K = 31
R = 15
OFF = 8
C = 16
Z = 128
W = 3 * C
HIGH = lax.Precision.HIGH

VM = pl.BlockSpec(memory_space=pltpu.VMEM)
SM = pl.BlockSpec(memory_space=pltpu.SMEM)


def call(body, outs, specs, scratch=(), flops=0, moved=0, vmem=48, grid=()):
    return pl.pallas_call(
        body,
        grid=grid,
        out_shape=[jax.ShapeDtypeStruct(s, jnp.float32) for s in outs],
        in_specs=specs,
        out_specs=[VM] * len(outs),
        scratch_shapes=list(scratch),
        compiler_params=pltpu.CompilerParams(vmem_limit_bytes=vmem << 20),
        cost_estimate=pl.CostEstimate(
            flops=flops, bytes_accessed=moved, transcendentals=0
        ),
    )


def edges(axis):
    place = lax.axis_index(axis)
    return place > 0, place < lax.axis_size(axis) - 1


def shift(block, axis, step):
    count = lax.axis_size(axis)
    return lax.ppermute(block, axis, [(i, (i + step) % count) for i in range(count)])


def lanes(rows):
    return lax.broadcasted_iota(jnp.int32, (rows, Z), 1)


def build_bands(line_y, line_z, flip_z, band_y, band_t, forward_z, backward_z):
    for view in range(V):
        row = jnp.broadcast_to(line_y[view : view + 1, :], (C, Z))
        band_y[view * C : (view + 1) * C, :] = pltpu.roll(
            row, 1, 1, stride=1, stride_axis=0
        )
        row = jnp.broadcast_to(flip_z[view : view + 1, :], (2 * Z, 2 * Z))
        forward_z[view] = pltpu.roll(row, 2 * Z - R, 1, stride=1, stride_axis=0)
        row = jnp.broadcast_to(line_z[view : view + 1, :], (2 * Z, 2 * Z))
        backward_z[view] = pltpu.roll(row, 2 * Z - R, 1, stride=1, stride_axis=0)[:, :Z]
    band_t[...] = band_y[...].T[:W, :]


def pack_rows(cover, raw, up, down):
    for view in range(V):
        up[view, :C] = raw[view, :, OFF:, :]
        down[view, :C] = raw[view, :, :OFF, :]
        level = jnp.full((OFF, Z), cover[view, 0].astype(jnp.float32))
        up[view, C] = level
        down[view, C] = level


def shift_rows(offsets, cover, raw, low, high, moved, up, down, wide):
    has_low, has_high = edges("by")
    row = lax.broadcasted_iota(jnp.int32, (C, Z), 0)
    for view in range(V):
        wide[view, :, 0:OFF, :] = jnp.where(has_low, low[view, :C], 0.0)
        wide[view, :, OFF : OFF + C, :] = raw[view]
        wide[view, :, OFF + C :, :] = jnp.where(has_high, high[view, :C], 0.0)
        block = wide[view, :, pl.ds(OFF + offsets[view, 1], C), :]
        moved[view] = block
        own = jnp.full((C, Z), cover[view, 0].astype(jnp.float32))
        below = jnp.where(has_low, low[view, C], 0.0)
        above = jnp.where(has_high, high[view, C], 0.0)
        below = jnp.concatenate([below, below], axis=0)
        above = jnp.concatenate([above, above], axis=0)
        tile = jnp.where(row == 0, below, jnp.where(row == 1, own, above))
        up[view, :OFF] = block[OFF:]
        down[view, :OFF] = block[:OFF]
        up[view, OFF] = tile
        down[view, OFF] = tile


def join_planes(low, own, high, wide):
    has_low, has_high = edges("bx")
    wide[0:C] = jnp.where(has_low, low[...], 0.0)
    wide[C : 2 * C] = own[...]
    wide[2 * C :] = jnp.where(has_high, high[...], 0.0)


def pack_lanes(block, first):
    lane = lanes(64)
    packed = None
    for group in range(4):
        piece = block[4 * group : 4 * group + 4].reshape(64, Z)
        turn = (32 * group - first) % Z
        if turn:
            piece = pltpu.roll(piece, turn, 1)
        packed = piece if packed is None else jnp.where(lane >= 32 * group, piece, packed)
    return packed


def forward(
    offsets, taps_x, band_y, own, low, high, cover, rows, rows_low, rows_high,
    blurred, shifted, up, down, tiles, planes, wide,
):
    has_low, has_high = edges("by")
    left, right = edges("bx")
    band = band_y[:, :W]
    for pair in range(W // 2):
        sides = []
        for a in (2 * pair, 2 * pair + 1):
            sides.append(
                jnp.concatenate(
                    [
                        jnp.where(has_low, low[a], 0.0),
                        own[a],
                        jnp.where(has_high, high[a], 0.0),
                    ],
                    axis=0,
                )
            )
        both = jnp.dot(
            band, jnp.concatenate(sides, axis=1), precision=HIGH,
            preferred_element_type=jnp.float32,
        )
        planes[2 * pair] = both[:, :Z]
        planes[2 * pair + 1] = both[:, Z:]

    @pl.loop(0, V)
    def _(view):
        taps = [jnp.full((8, Z), taps_x[view * K + t]) for t in range(K)]
        for half in range(2):
            sums = [None] * C
            for a in range(1, W - 1):
                plane = planes[a, pl.ds(pl.multiple_of(view * C + 8 * half, 8), 8), :]
                for i in range(C):
                    t = a - i - 1
                    if 0 <= t < K:
                        term = taps[t] * plane
                        sums[i] = term if sums[i] is None else sums[i] + term
            for i in range(C):
                blurred[view, i, 8 * half : 8 * half + 8, :] = sums[i]
        block = blurred[view]
        up[view] = pack_lanes(block, 96)
        down[view] = pack_lanes(block, 0)
        wide[0:OFF] = jnp.where(left, rows_low[view, :OFF], 0.0)
        wide[OFF : OFF + C] = rows[view]
        wide[OFF + C :] = jnp.where(right, rows_high[view, :OFF], 0.0)
        block = wide[pl.ds(OFF + offsets[view, 0], C)]
        shifted[view] = block
        up[V + view] = pack_lanes(block, 96)
        down[V + view] = pack_lanes(block, 0)

    lane = lanes(8)
    up[2 * V] = jnp.zeros((64, Z), jnp.float32)
    down[2 * V] = jnp.zeros((64, Z), jnp.float32)
    for view in range(V):
        below = jnp.where(left, rows_low[view, OFF, :8], 0.0)
        above = jnp.where(right, rows_high[view, OFF, :8], 0.0)
        middle = cover[view, OFF, :8]
        tile = jnp.where(lane == 0, below, jnp.where(lane == 1, middle, above))
        up[2 * V, 8 * view : 8 * view + 8] = tile
        down[2 * V, 8 * view : 8 * view + 8] = tile
        tiles[8 * view : 8 * view + 8] = tile


def ring(block, low, high, has_low, has_high):
    lane = lanes(64)
    sides = []
    for group in range(4):
        before = pltpu.roll(low, 96 - 32 * group, 1) if group < 3 else low
        after = pltpu.roll(high, (Z - 32 * group) % Z, 1) if group else high
        before = jnp.where(jnp.logical_and(lane >= 96, has_low), before, 0.0)
        after = jnp.where(jnp.logical_and(lane < 32, has_high), after, 0.0)
        sides.append(before + after)
    return jnp.concatenate([block, jnp.concatenate(sides, axis=0)], axis=1)


def ratio_back(
    offsets, taps_x, band_t, forward_z, backward_z, blurred, shifted, low, high, tiles,
    out_low, out_mid, out_high, spread, planes,
):
    has_low, has_high = edges("bz")
    lane = lax.broadcasted_iota(jnp.int32, (1, 2 * Z), 1)

    @pl.loop(0, V)
    def _(view):
        block = ring(
            blurred[view].reshape(C * C, Z), low[view], high[view], has_low, has_high
        )
        model = jnp.dot(
            block, forward_z[view], precision=HIGH, preferred_element_type=jnp.float32
        )
        seen = ring(
            shifted[view].reshape(C * C, Z), low[V + view], high[V + view],
            has_low, has_high,
        )
        seen = pltpu.roll(seen, lax.rem(2 * Z - offsets[view, 2], 2 * Z), 1)
        row = pl.ds(pl.multiple_of(view * 8, 8), 8)
        own = jnp.broadcast_to(tiles[row, :][1:2, 1:2], (1, 2 * Z))
        after = jnp.broadcast_to(high[2 * V, row, :][1:2, 1:2], (1, 2 * Z))
        before = jnp.broadcast_to(low[2 * V, row, :][1:2, 1:2], (1, 2 * Z))
        after = jnp.where(jnp.logical_and(lane < Z + R, has_high), after, 0.0)
        before = jnp.where(
            jnp.logical_and(lane >= 2 * Z - R, has_low), before, 0.0
        )
        mask = jnp.where(lane < Z, own, after + before)
        ratio = jnp.where(mask > 0.0, mask * seen / model, 0.0)
        back = jnp.dot(
            ratio, backward_z[view], precision=HIGH, preferred_element_type=jnp.float32
        )
        spread[...] = back.reshape(C, C, Z)
        taps = [jnp.full((8, Z), taps_x[view * K + t]) for t in range(K)]
        for half in range(2):
            source = [spread[i, 8 * half : 8 * half + 8, :] for i in range(C)]
            for a in range(1, W - 1):
                total = None
                for i in range(C):
                    t = a - i - 1
                    if 0 <= t < K:
                        term = taps[t] * source[i]
                        total = term if total is None else total + term
                planes[a, pl.ds(pl.multiple_of(view * C + 8 * half, 8), 8), :] = total

    planes[0] = jnp.zeros((V * C, Z), jnp.float32)
    planes[W - 1] = jnp.zeros((V * C, Z), jnp.float32)
    for pair in range(W // 2):
        both = jnp.concatenate([planes[2 * pair], planes[2 * pair + 1]], axis=1)
        both = jnp.dot(
            band_t[...], both, precision=HIGH, preferred_element_type=jnp.float32
        )
        for side in range(2):
            part = both[:, side * Z : (side + 1) * Z]
            out_low[2 * pair + side] = part[:C]
            out_mid[2 * pair + side] = part[C : 2 * C]
            out_high[2 * pair + side] = part[2 * C :]


def add_rows(mid, from_low, from_high, out_low, out_mid, out_high):
    has_low, has_high = edges("by")
    total = (
        mid[...]
        + jnp.where(has_low, from_low[...], 0.0)
        + jnp.where(has_high, from_high[...], 0.0)
    )
    out_low[...] = total[:C]
    out_mid[...] = total[C : 2 * C]
    out_high[...] = total[2 * C :]


def weigh(part_x, part_y, part_z, tiles, low, high, weights):
    has_low, has_high = edges("bz")
    sums = [jnp.zeros((C, Z), jnp.float32) for _ in range(C)]
    for view in range(V):
        row = slice(8 * view, 8 * view + 8)
        near = [
            jnp.where(has_low, low[0, row], 0.0),
            tiles[row],
            jnp.where(has_high, high[0, row], 0.0),
        ]
        for p in range(3):
            term = None
            for r in range(3):
                level = None
                for q in range(3):
                    cell = jnp.broadcast_to(near[r][q : q + 1, p : p + 1], (C, Z))
                    cell = cell * part_y[view, q]
                    level = cell if level is None else level + cell
                level = level * part_z[view, r : r + 1, :]
                term = level if term is None else term + level
            for i in range(C):
                sums[i] = sums[i] + part_x[(view * C + i) * 3 + p] * term
    for i in range(C):
        weights[i] = sums[i]


def finish(estimate, mid, from_low, from_high, weights, out):
    has_low, has_high = edges("bx")
    total = (
        mid[...]
        + jnp.where(has_low, from_low[...], 0.0)
        + jnp.where(has_high, from_high[...], 0.0)
    )
    out[...] = estimate[...] * total / weights[...]


def block_parts(taps, count):
    cell = jnp.arange(count)[:, None]
    tap = jnp.arange(K)[None, :]
    before = (tap > cell + R).astype(jnp.float32)
    after = (tap < cell + R + 1 - count).astype(jnp.float32)
    which = jnp.stack([before, 1.0 - before - after, after])
    return jnp.einsum("vt,pit->vip", taps, which, precision=lax.Precision.HIGHEST)


def on_device(estimate, raw, psf, offsets, coverage):
    taps = psf / jnp.sum(psf, axis=2, keepdims=True)
    taps_x = taps[:, 0].reshape(V * K)
    line_y = jnp.pad(taps[:, 1], ((0, 0), (0, Z - K)))
    line_z = jnp.pad(taps[:, 2], ((0, 0), (0, 2 * Z - K)))
    flip_z = jnp.pad(jnp.flip(taps[:, 2], 1), ((0, 0), (0, 2 * Z - K)))
    part_x = block_parts(taps[:, 0], C).reshape(V * C * 3)
    part_y = jnp.broadcast_to(
        block_parts(taps[:, 1], C).transpose(0, 2, 1)[..., None], (V, 3, C, Z)
    )
    part_z = block_parts(taps[:, 2], Z).transpose(0, 2, 1)
    cover = coverage.reshape(V, 1)

    left = shift(estimate, "bx", 1)
    right = shift(estimate, "bx", -1)
    up, down = call(
        pack_rows, [(V, C + 1, OFF, Z)] * 2, [SM, VM], moved=3 << 19
    )(cover, raw)
    rows_low = shift(up, "by", 1)
    rows_high = shift(down, "by", -1)
    band_y, band_t, forward_z, backward_z = call(
        build_bands,
        [(V * C, Z), (W, V * C), (V, 2 * Z, 2 * Z), (V, 2 * Z, Z)],
        [VM, VM, VM],
        moved=3 << 20,
    )(line_y, line_z, flip_z)
    (wide,) = call(join_planes, [(W, C, Z)], [VM] * 3, moved=3 << 18)(
        left, estimate, right
    )
    low = shift(wide, "by", 1)
    high = shift(wide, "by", -1)
    moved, up, down = call(
        shift_rows,
        [(V, C, C, Z), (V, OFF + 1, C, Z), (V, OFF + 1, C, Z)],
        [SM, SM, VM, VM, VM],
        [pltpu.VMEM((V, C, 2 * C, Z), jnp.float32)],
        moved=3 << 20,
    )(offsets, cover, raw, rows_low, rows_high)
    shifted_low = shift(up, "bx", 1)
    shifted_high = shift(down, "bx", -1)
    blurred, shifted, pack_up, pack_down, tiles = call(
        forward,
        [
            (V, C, C, Z),
            (V, C, C, Z),
            (2 * V + 1, 64, Z),
            (2 * V + 1, 64, Z),
            (V * 8, Z),
        ],
        [SM, SM] + [VM] * 8,
        [
            pltpu.VMEM((W, V * C, Z), jnp.float32),
            pltpu.VMEM((2 * C, C, Z), jnp.float32),
        ],
        flops=1 << 28,
        moved=6 << 20,
    )(offsets, taps_x, band_y, wide, low, high, up, moved, shifted_low, shifted_high)
    from_low = shift(pack_up, "bz", 1)
    from_high = shift(pack_down, "bz", -1)
    out_low, out_mid, out_high = call(
        ratio_back,
        [(W, C, Z)] * 3,
        [SM, SM] + [VM] * 8,
        [
            pltpu.VMEM((C, C, Z), jnp.float32),
            pltpu.VMEM((W, V * C, Z), jnp.float32),
        ],
        flops=1 << 29,
        moved=8 << 20,
    )(
        offsets, taps_x, band_t, forward_z, backward_z, blurred, shifted,
        from_low, from_high, tiles,
    )
    sum_low = shift(out_high, "by", 1)
    sum_high = shift(out_low, "by", -1)
    last = pl.BlockSpec((1, 64, Z), lambda i: (2 * V, 0, 0))
    (weights,) = call(
        weigh, [(C, C, Z)], [SM, VM, VM, VM, last, last], moved=1 << 19, grid=(1,)
    )(part_x, part_y, part_z, tiles, from_low, from_high)
    out_low, out_mid, out_high = call(
        add_rows, [(C, C, Z)] * 3, [VM] * 3, moved=3 << 19
    )(out_mid, sum_low, sum_high)
    sum_low = shift(out_high, "bx", 1)
    sum_high = shift(out_low, "bx", -1)
    (out,) = call(finish, [(C, C, Z)], [VM] * 5, moved=3 << 18)(
        estimate, out_mid, sum_low, sum_high, weights
    )
    return out


def solution(mesh):
    return jax.shard_map(
        on_device,
        mesh=mesh,
        in_specs=(
            P("bx", "by", "bz"),
            P(None, "bx", "by", "bz"),
            P(),
            P(),
            P(None, "bx", "by", "bz"),
        ),
        out_specs=P("bx", "by", "bz"),
        check_vma=False,
    )
```

```python
import jax
import jax.numpy as jnp
from jax import lax
from jax.experimental import pallas as pl
from jax.experimental.pallas import tpu as pltpu
from jax.sharding import PartitionSpec as P

V = 6
K = 31
R = 15
OFF = 8
C = 16
Z = 128
W = 3 * C
HIGH = lax.Precision.HIGH
HIGHEST = lax.Precision.HIGHEST
F32 = jnp.float32

VM = pl.BlockSpec(memory_space=pltpu.VMEM)
SM = pl.BlockSpec(memory_space=pltpu.SMEM)
ANY = pl.BlockSpec(memory_space=pl.ANY)
HBM = pl.BlockSpec(memory_space=pltpu.HBM)


def call(
    body, outs, specs, scratch=(), out_specs=None, grid=(), alias=None,
    flops=0, moved=0, vmem=16,
):
    return pl.pallas_call(
        body,
        grid=grid,
        out_shape=[jax.ShapeDtypeStruct(s, F32) for s in outs],
        in_specs=specs,
        out_specs=out_specs or [VM] * len(outs),
        scratch_shapes=list(scratch),
        input_output_aliases=alias or {},
        compiler_params=pltpu.CompilerParams(vmem_limit_bytes=vmem << 20),
        cost_estimate=pl.CostEstimate(
            flops=flops, bytes_accessed=moved, transcendentals=0
        ),
    )


def edges(axis):
    place = lax.axis_index(axis)
    return place > 0, place < lax.axis_size(axis) - 1


def even():
    return lax.rem(lax.axis_index("bz"), 2) == 0


def shift(block, axis, step):
    count = lax.axis_size(axis)
    return lax.ppermute(block, axis, [(i, (i + step) % count) for i in range(count)])


def swap(block, first):
    count = lax.axis_size("bz")
    pairs = []
    for i in range(first, count, 2):
        a, b = i % count, (i + 1) % count
        pairs += [(a, b), (b, a)]
    return lax.ppermute(block, "bz", pairs)


def lanes(rows):
    return lax.broadcasted_iota(jnp.int32, (rows, Z), 1)


def dot(a, b, precision=HIGH):
    return jnp.dot(a, b, precision=precision, preferred_element_type=F32)


def pack_planes(cover, raw, up, down, flags, sem):
    tag = pltpu.make_async_copy(cover, flags, sem)
    tag.start()
    up[:, :OFF] = raw[:, OFF:]
    down[:, :OFF] = raw[:, :OFF]
    tag.wait()
    for view in range(V):
        tile = jnp.full((C, Z), flags[view].astype(F32))
        up[view, OFF] = tile
        down[view, OFF] = tile


def build(
    offsets, psf, after, norm, table, band_y, band_t, forward_z, backward_z
):
    norm[...] = jnp.zeros((3, 8, Z), F32)
    for view in range(V):
        for axis in range(3):
            line = psf[view, axis : axis + 1, :]
            norm[axis, view : view + 1, 0:K] = line / jnp.sum(
                line, axis=1, keepdims=True
            )
    for view in range(V):
        line = norm[0, view : view + 1, :]
        for t in range(K):
            table[view, t] = jnp.broadcast_to(line[:, t : t + 1], (8, Z))
        row = jnp.broadcast_to(norm[1, view : view + 1, :], (C, Z))
        band_y[view * C : (view + 1) * C, :] = pltpu.roll(
            row, 1, 1, stride=1, stride_axis=0
        )
        row = norm[2, view : view + 1, :]
        row = jnp.concatenate([row, jnp.zeros((1, Z), F32)], axis=1)
        row = jnp.broadcast_to(row, (2 * Z, 2 * Z))
        band = pltpu.roll(row, 2 * Z - R, 1, stride=1, stride_axis=0)
        band = pltpu.roll(band, lax.rem(2 * Z - offsets[2, view], 2 * Z), 1)
        backward_z[view] = band[:, :Z]
        forward_z[view] = band[:Z, :].T
    band_t[...] = band_y[...].T[:W, :]


def join_planes(low, own, high, wide, sem):
    copy = pltpu.make_async_copy(own, wide.at[pl.ds(C, C)], sem)
    copy.start()
    has_low, has_high = edges("bx")
    wide[0:C] = jnp.where(has_low, low[...], 0.0)
    wide[2 * C :] = jnp.where(has_high, high[...], 0.0)
    copy.wait()


def pack_lanes(block, first):
    lane = lanes(64)
    packed = None
    for group in range(4):
        piece = block[4 * group : 4 * group + 4].reshape(64, Z)
        turn = (32 * group - first) % Z
        if turn:
            piece = pltpu.roll(piece, turn, 1)
        packed = piece if packed is None else jnp.where(lane >= 32 * group, piece, packed)
    return packed


def pack_sides(block, near, far, view):
    up = pack_lanes(block, 96)
    down = pack_lanes(block, 0)
    near[view, :64] = jnp.where(even(), up, down)
    far[view, :64] = jnp.where(even(), down, up)


def forward(table, band_y, own, low, high, cover, after, blurred, near, far, planes):
    has_low, has_high = edges("by")
    band = band_y[:, :W]
    for pair in range(W // 2):
        sides = []
        for a in (2 * pair, 2 * pair + 1):
            sides.append(
                jnp.concatenate(
                    [
                        jnp.where(has_low, low[a], 0.0),
                        own[a],
                        jnp.where(has_high, high[a], 0.0),
                    ],
                    axis=0,
                )
            )
        both = dot(band, jnp.concatenate(sides, axis=1))
        planes[2 * pair] = both[:, :Z]
        planes[2 * pair + 1] = both[:, Z:]

    @pl.loop(0, V)
    def _(view):
        taps = [table[view, t] for t in range(K)]
        for half in range(2):
            sums = [None] * C
            for a in range(1, W - 1):
                plane = planes[a, pl.ds(pl.multiple_of(view * C + 8 * half, 8), 8), :]
                for i in range(C):
                    t = a - i - 1
                    if 0 <= t < K:
                        term = taps[t] * plane
                        sums[i] = term if sums[i] is None else sums[i] + term
            for i in range(C):
                blurred[view, i, 8 * half : 8 * half + 8, :] = sums[i]
        pack_sides(blurred[view], near, far, view)

    for view in range(V):
        tile = jnp.full((8, Z), cover[view].astype(F32))
        near[view, 64:] = tile
        far[view, 64:] = tile


def ring(block, near, far):
    has_low, has_high = edges("bz")
    lane = lanes(64)
    low = jnp.where(even(), far, near)
    high = jnp.where(even(), near, far)
    sides = []
    for group in range(4):
        before = pltpu.roll(low, 96 - 32 * group, 1) if group < 3 else low
        after = pltpu.roll(high, (Z - 32 * group) % Z, 1) if group else high
        before = jnp.where(jnp.logical_and(lane >= 96, has_low), before, 0.0)
        after = jnp.where(jnp.logical_and(lane < 32, has_high), after, 0.0)
        sides.append(before + after)
    return jnp.concatenate([block, jnp.concatenate(sides, axis=0)], axis=1)


def shift_planes(
    offsets, cover, raw, low, high, after, shifted, up, down, tiles, wide
):
    has_low, has_high = edges("bx")
    lane = lanes(8)
    for view in range(V):
        wide[view, 0:OFF] = jnp.where(has_low, low[view, :OFF], 0.0)
        wide[view, OFF : OFF + C] = raw[view]
        wide[view, OFF + C :] = jnp.where(has_high, high[view, :OFF], 0.0)
        block = wide[view, pl.ds(OFF + offsets[0, view], C)]
        shifted[view, :, OFF : OFF + C] = block
        up[view, :C] = block[:, OFF:]
        down[view, :C] = block[:, :OFF]
        below = jnp.where(has_low, low[view, OFF, 0:8], 0.0)
        above = jnp.where(has_high, high[view, OFF, 0:8], 0.0)
        own = jnp.full((8, Z), cover[view].astype(F32))
        tile = jnp.where(lane == 0, below, jnp.where(lane == 1, own, above))
        tiles[view] = tile
        up[view, C] = tile
        down[view, C] = tile


def shift_rows(offsets, held, low, high, tiles, after, out, marks, main):
    has_low, has_high = edges("by")
    lane = lanes(8)
    for view in range(V):
        main[view, :, 0:OFF] = jnp.where(has_low, low[view, :C], 0.0)
        main[view, :, OFF + C :] = jnp.where(has_high, high[view, :C], 0.0)
        out[view] = main[view, :, pl.ds(OFF + offsets[1, view], C)]
        below = jnp.where(has_low, low[view, C], 0.0)
        above = jnp.where(has_high, high[view, C], 0.0)
        middle = pltpu.roll(tiles[view], 3, 1)
        above = pltpu.roll(above, 6, 1)
        marks[view] = jnp.where(lane < 3, below, jnp.where(lane < 6, middle, above))


def divide(
    offsets, cover, forward_z, blurred, low, high, seen, marks, ratio, near, far
):
    has_low, has_high = edges("bz")
    lane = lanes(1)
    for view in range(V):
        block = ring(
            blurred[view].reshape(C * C, Z), low[view, :64], high[view, :64]
        )
        model = dot(block, forward_z[view]).reshape(C, C, Z)
        before = jnp.where(even(), high[view, 64:65], low[view, 64:65])
        after = jnp.where(even(), low[view, 64:65], high[view, 64:65])
        before = jnp.where(has_low, before, 0.0)
        after = jnp.where(has_high, after, 0.0)
        own = jnp.full((1, Z), cover[view].astype(F32))
        place = lane - offsets[2, view]
        mask = jnp.where(place < 0, before, jnp.where(place < Z, own, after))
        block = jnp.where(mask > 0.0, mask * seen[view] / model, 0.0)
        ratio[view] = block
        pack_sides(block, near, far, view)
        near[view, 64:] = marks[view]
        far[view, 64:] = marks[view]


def ratio_back(
    table, band_t, backward_z, ratio, low, high, out_low, out_mid, out_high, planes
):
    @pl.loop(0, V)
    def _(view):
        block = ring(ratio[view].reshape(C * C, Z), low[view, :64], high[view, :64])
        back = dot(block, backward_z[view]).reshape(C, C, Z)
        taps = [table[view, t] for t in range(K)]
        for half in range(2):
            source = [back[i, 8 * half : 8 * half + 8, :] for i in range(C)]
            for a in range(1, W - 1):
                total = None
                for i in range(C):
                    t = a - i - 1
                    if 0 <= t < K:
                        term = taps[t] * source[i]
                        total = term if total is None else total + term
                planes[a, pl.ds(pl.multiple_of(view * C + 8 * half, 8), 8), :] = total

    planes[0] = jnp.zeros((V * C, Z), F32)
    planes[W - 1] = jnp.zeros((V * C, Z), F32)
    for pair in range(W // 2):
        both = jnp.concatenate([planes[2 * pair], planes[2 * pair + 1]], axis=1)
        both = dot(band_t[...], both)
        for part in range(2):
            piece = both[:, part * Z : (part + 1) * Z]
            out_low[2 * pair + part] = piece[:C]
            out_mid[2 * pair + part] = piece[C : 2 * C]
            out_high[2 * pair + part] = piece[2 * C :]


def add_rows(mid, from_low, from_high, out_low, out_mid, out_high):
    has_low, has_high = edges("by")
    total = (
        mid[...]
        + jnp.where(has_low, from_low[...], 0.0)
        + jnp.where(has_high, from_high[...], 0.0)
    )
    out_low[...] = total[:C]
    out_mid[...] = total[C : 2 * C]
    out_high[...] = total[2 * C :]


def part(tap, cell, count, which):
    before = jnp.where(tap > cell + R, 1.0, 0.0)
    after = jnp.where(tap < cell + R + 1 - count, 1.0, 0.0)
    return jnp.where(which == 0, before, jnp.where(which == 2, after, 1.0 - before - after))


def weigh(norm, marks, near_marks, far_marks, weights):
    has_low, has_high = edges("bz")
    tap = lax.broadcasted_iota(jnp.int32, (Z, Z), 0)
    cell = lax.broadcasted_iota(jnp.int32, (Z, Z), 1)
    part_x = [dot(norm[0], part(tap, cell, C, p), HIGHEST) for p in range(3)]
    part_z = [dot(norm[2], part(tap, cell, Z, r), HIGHEST) for r in range(3)]
    part_y = [dot(norm[1], part(tap, cell, C, q), HIGHEST) for q in range(3)]
    part_y = [jnp.concatenate([y] * C, axis=0).T for y in part_y]
    sums = [jnp.zeros((C, Z), F32) for _ in range(C)]
    for view in range(V):
        low = jnp.where(even(), far_marks[view, 0:1], near_marks[view, 0:1])
        high = jnp.where(even(), near_marks[view, 0:1], far_marks[view, 0:1])
        near = [
            jnp.where(has_low, low, 0.0),
            marks[view, 0:1],
            jnp.where(has_high, high, 0.0),
        ]
        share = [
            jnp.broadcast_to(part_y[q][:C, view : view + 1], (C, Z)) for q in range(3)
        ]
        for p in range(3):
            term = None
            for r in range(3):
                level = None
                for q in range(3):
                    at = 3 * q + p
                    cell = jnp.broadcast_to(near[r][:, at : at + 1], (C, Z)) * share[q]
                    level = cell if level is None else level + cell
                level = level * part_z[r][view : view + 1, :]
                term = level if term is None else term + level
            for i in range(C):
                scale = jnp.broadcast_to(part_x[p][view : view + 1, i : i + 1], (C, Z))
                sums[i] = sums[i] + scale * term
    for i in range(C):
        weights[i] = sums[i]


def finish(estimate, mid, from_low, from_high, weights, out):
    has_low, has_high = edges("bx")
    total = (
        mid[...]
        + jnp.where(has_low, from_low[...], 0.0)
        + jnp.where(has_high, from_high[...], 0.0)
    )
    out[...] = estimate[...] * total / weights[...]


def on_device(estimate, raw, psf, offsets, coverage):
    cover = coverage.reshape(V)
    offsets = offsets.T
    full = (V, C, C, Z)

    left = shift(estimate, "bx", 1)
    right = shift(estimate, "bx", -1)
    up, down = call(
        pack_planes,
        [(V, OFF + 1, C, Z)] * 2,
        [HBM, VM],
        [pltpu.SMEM((V,), jnp.int32), pltpu.SemaphoreType.DMA],
        moved=3 << 19,
    )(cover, raw)
    raw_low = shift(up, "bx", 1)
    raw_high = shift(down, "bx", -1)
    (wide,) = call(
        join_planes,
        [(W, C, Z)],
        [VM, HBM, VM],
        [pltpu.SemaphoreType.DMA],
        moved=1 << 18,
    )(left, estimate, right)
    norm, table, band_y, band_t, forward_z, backward_z = call(
        build,
        [
            (3, 8, Z),
            (V, K, 8, Z),
            (V * C, Z),
            (W, V * C),
            (V, 2 * Z, Z),
            (V, 2 * Z, Z),
        ],
        [SM, VM, ANY],
        moved=1 << 23,
    )(offsets, psf, wide)
    low = shift(wide, "by", 1)
    high = shift(wide, "by", -1)

    shifted, up, down, tiles = call(
        shift_planes,
        [
            (V, C, 2 * C, Z),
            (V, C + 1, OFF, Z),
            (V, C + 1, OFF, Z),
            (V, 8, Z),
        ],
        [SM, SM, VM, VM, VM, ANY],
        [pltpu.VMEM((V, 2 * C, C, Z), F32)],
        moved=1 << 26,
    )(offsets, cover, raw, raw_low, raw_high, norm)
    raw_low = shift(up, "by", 1)
    raw_high = shift(down, "by", -1)

    blurred, near, far = call(
        forward,
        [full, (V, 72, Z), (V, 72, Z)],
        [VM] * 5 + [SM, ANY],
        [pltpu.VMEM((W, V * C, Z), F32)],
        flops=1 << 34,
        moved=1 << 26,
    )(table, band_y, wide, low, high, cover, tiles)
    near, far = swap(near, 0), swap(far, 1)

    seen, marks, _ = call(
        shift_rows,
        [full, (V, 8, Z), (V, C, 2 * C, Z)],
        [SM] + [VM] * 4 + [ANY],
        alias={1: 2},
        moved=1 << 26,
    )(offsets, shifted, raw_low, raw_high, tiles, blurred)

    ratio, near, far = call(
        divide,
        [full, (V, 72, Z), (V, 72, Z)],
        [SM, SM] + [VM] * 6,
        flops=1 << 34,
        moved=1 << 26,
    )(offsets, cover, forward_z, blurred, near, far, seen, marks)
    near, far = swap(near, 0), swap(far, 1)

    out_low, out_mid, out_high = call(
        ratio_back,
        [(W, C, Z)] * 3,
        [VM] * 6,
        [pltpu.VMEM((W, V * C, Z), F32)],
        flops=1 << 34,
        moved=8 << 20,
    )(table, band_t, backward_z, ratio, near, far)
    sum_low = shift(out_high, "by", 1)
    sum_high = shift(out_low, "by", -1)
    last = pl.BlockSpec((V, 8, Z), lambda i: (0, 8, 0))
    (weights,) = call(
        weigh, [(C, C, Z)], [VM, VM, last, last], grid=(1,), moved=1 << 19
    )(norm, marks, near, far)
    out_low, out_mid, out_high = call(
        add_rows, [(C, C, Z)] * 3, [VM] * 3, moved=3 << 19
    )(out_mid, sum_low, sum_high)
    sum_low = shift(out_high, "bx", 1)
    sum_high = shift(out_low, "bx", -1)
    (out,) = call(finish, [(C, C, Z)], [VM] * 5, moved=3 << 18)(
        estimate, out_mid, sum_low, sum_high, weights
    )
    return out


def solution(mesh):
    return jax.shard_map(
        on_device,
        mesh=mesh,
        in_specs=(
            P("bx", "by", "bz"),
            P(None, "bx", "by", "bz"),
            P(),
            P(),
            P(None, "bx", "by", "bz"),
        ),
        out_specs=P("bx", "by", "bz"),
        check_vma=False,
    )
```

```python
import jax
import jax.numpy as jnp
from jax import lax
from jax.experimental import pallas as pl
from jax.experimental.pallas import tpu as pltpu
from jax.sharding import PartitionSpec as P

V = 6
K = 31
R = 15
OFF = 8
C = 16
Z = 128
W = 3 * C
HIGH = lax.Precision.HIGH
HIGHEST = lax.Precision.HIGHEST
F32 = jnp.float32
BF16 = jnp.bfloat16

VM = pl.BlockSpec(memory_space=pltpu.VMEM)
SM = pl.BlockSpec(memory_space=pltpu.SMEM)
ANY = pl.BlockSpec(memory_space=pl.ANY)
HBM = pl.BlockSpec(memory_space=pltpu.HBM)


def call(
    body, outs, specs, scratch=(), out_specs=None, grid=(), alias=None,
    flops=0, moved=0, vmem=16,
):
    return pl.pallas_call(
        body,
        grid=grid,
        out_shape=[
            s if hasattr(s, "dtype") else jax.ShapeDtypeStruct(s, F32) for s in outs
        ],
        in_specs=specs,
        out_specs=out_specs or [VM] * len(outs),
        scratch_shapes=list(scratch),
        input_output_aliases=alias or {},
        compiler_params=pltpu.CompilerParams(vmem_limit_bytes=vmem << 20),
        cost_estimate=pl.CostEstimate(
            flops=flops, bytes_accessed=moved, transcendentals=0
        ),
    )


def edges(axis):
    place = lax.axis_index(axis)
    return place > 0, place < lax.axis_size(axis) - 1


def even():
    return lax.rem(lax.axis_index("bz"), 2) == 0


def shift(block, axis, step):
    count = lax.axis_size(axis)
    return lax.ppermute(block, axis, [(i, (i + step) % count) for i in range(count)])


def swap(block, first):
    count = lax.axis_size("bz")
    pairs = []
    for i in range(first, count, 2):
        a, b = i % count, (i + 1) % count
        pairs += [(a, b), (b, a)]
    return lax.ppermute(block, "bz", pairs)


def lanes(rows):
    return lax.broadcasted_iota(jnp.int32, (rows, Z), 1)


def dot(a, b, precision=HIGH):
    return jnp.dot(a, b, precision=precision, preferred_element_type=F32)


def split(block):
    high = block.astype(BF16)
    return high, (block - high.astype(F32)).astype(BF16)


def pack_planes(cover, raw, up, down, flags, sem):
    tag = pltpu.make_async_copy(cover, flags, sem)
    tag.start()
    up[:, :OFF] = raw[:, OFF:]
    down[:, :OFF] = raw[:, :OFF]
    tag.wait()
    for view in range(V):
        tile = jnp.full((C, Z), flags[view].astype(F32))
        up[view, OFF] = tile
        down[view, OFF] = tile


def build(
    offsets, psf, after, norm, table, fan_in, fan_out, fan_pair,
    forward_z, backward_z,
):
    norm[...] = jnp.zeros((3, 8, Z), F32)
    for view in range(V):
        for axis in range(3):
            line = psf[view, axis : axis + 1, :]
            norm[axis, view : view + 1, 0:K] = line / jnp.sum(
                line, axis=1, keepdims=True
            )
    bands = []
    for view in range(V):
        line = norm[0, view : view + 1, :]
        for t in range(K):
            table[view, t] = jnp.broadcast_to(line[:, t : t + 1], (8, Z))
        row = jnp.broadcast_to(norm[1, view : view + 1, :], (C, Z))
        bands.append(pltpu.roll(row, 1, 1, stride=1, stride_axis=0))
        row = norm[2, view : view + 1, :]
        row = jnp.concatenate([row, jnp.zeros((1, Z), F32)], axis=1)
        row = jnp.broadcast_to(row, (2 * Z, 2 * Z))
        band = pltpu.roll(row, 2 * Z - R, 1, stride=1, stride_axis=0)
        band = pltpu.roll(band, lax.rem(2 * Z - offsets[2, view], 2 * Z), 1)
        backward_z[view] = band[:, :Z]
        forward_z[view] = band[:Z, :].T
    def side_by_side(*parts):
        total = None
        for turn, block in parts:
            block = block.astype(F32)
            block = jnp.concatenate([block, jnp.zeros_like(block)], axis=1)
            block = pltpu.roll(block, turn, 1) if turn else block
            total = block if total is None else total + block
        return total.astype(BF16)

    high, low = split(jnp.concatenate(bands, axis=0))
    fan_in[...] = side_by_side((0, high), (W, high), (2 * W, low))
    for out, order in ((fan_out, range(V)), (fan_pair, (0, 2, 4, 1, 3, 5))):
        rows = [bands[v] for v in order]
        rows += [jnp.zeros((Z - V * C, Z), F32)]
        high, low = split(jnp.concatenate(rows, axis=0).T[:W, :])
        out[0:W] = side_by_side((0, high), (V * C, high))
        out[W:] = side_by_side((0, low), (V * C, low))


def join_planes(low, own, high, wide, sem):
    copy = pltpu.make_async_copy(own, wide.at[pl.ds(C, C)], sem)
    copy.start()
    has_low, has_high = edges("bx")
    wide[0:C] = jnp.where(has_low, low[...], 0.0)
    wide[2 * C :] = jnp.where(has_high, high[...], 0.0)
    copy.wait()


def pack_lanes(block, first):
    lane = lanes(64)
    packed = None
    for group in range(4):
        piece = block[4 * group : 4 * group + 4].reshape(64, Z)
        turn = (32 * group - first) % Z
        if turn:
            piece = pltpu.roll(piece, turn, 1)
        packed = piece if packed is None else jnp.where(lane >= 32 * group, piece, packed)
    return packed


def pack_sides(block, near, far, view):
    up = pack_lanes(block, 96)
    down = pack_lanes(block, 0)
    near[view, :64] = jnp.where(even(), up, down)
    far[view, :64] = jnp.where(even(), down, up)


def forward(table, fan_in, own, low, high, cover, after, blurred, near, far, planes):
    has_low, has_high = edges("by")
    fan = fan_in[:, : 3 * W]
    for pair in range(W // 2):
        sides = []
        for a in (2 * pair, 2 * pair + 1):
            sides.append(
                jnp.concatenate(
                    [
                        jnp.where(has_low, low[a], 0.0),
                        own[a],
                        jnp.where(has_high, high[a], 0.0),
                    ],
                    axis=0,
                )
            )
        top, rest = split(jnp.concatenate(sides, axis=1))
        both = dot(fan, jnp.concatenate([top, rest, top], axis=0), None)
        planes[2 * pair] = both[:, :Z]
        planes[2 * pair + 1] = both[:, Z:]

    @pl.loop(0, V)
    def _(view):
        taps = [table[view, t] for t in range(K)]
        for half in range(2):
            sums = [None] * C
            for a in range(1, W - 1):
                plane = planes[a, pl.ds(pl.multiple_of(view * C + 8 * half, 8), 8), :]
                for i in range(C):
                    t = a - i - 1
                    if 0 <= t < K:
                        term = taps[t] * plane
                        sums[i] = term if sums[i] is None else sums[i] + term
            for i in range(C):
                blurred[view, i, 8 * half : 8 * half + 8, :] = sums[i]
        pack_sides(blurred[view], near, far, view)

    for view in range(V):
        tile = jnp.full((8, Z), cover[view].astype(F32))
        near[view, 64:] = tile
        far[view, 64:] = tile


def sides(near, far):
    has_low, has_high = edges("bz")
    lane = lanes(64)
    low = jnp.where(even(), far, near)
    high = jnp.where(even(), near, far)
    parts = []
    for group in range(4):
        before = pltpu.roll(low, 96 - 32 * group, 1) if group < 3 else low
        after = pltpu.roll(high, (Z - 32 * group) % Z, 1) if group else high
        before = jnp.where(jnp.logical_and(lane >= 96, has_low), before, 0.0)
        after = jnp.where(jnp.logical_and(lane < 32, has_high), after, 0.0)
        parts.append(before + after)
    return jnp.concatenate(parts, axis=0)


def shift_planes(
    offsets, cover, raw, low, high, after, shifted, up, down, tiles, wide
):
    has_low, has_high = edges("bx")
    lane = lanes(8)
    for view in range(V):
        wide[view, 0:OFF] = jnp.where(has_low, low[view, :OFF], 0.0)
        wide[view, OFF : OFF + C] = raw[view]
        wide[view, OFF + C :] = jnp.where(has_high, high[view, :OFF], 0.0)
        block = wide[view, pl.ds(OFF + offsets[0, view], C)]
        shifted[view, :, OFF : OFF + C] = block
        up[view, :C] = block[:, OFF:]
        down[view, :C] = block[:, :OFF]
        below = jnp.where(has_low, low[view, OFF, 0:8], 0.0)
        above = jnp.where(has_high, high[view, OFF, 0:8], 0.0)
        own = jnp.full((8, Z), cover[view].astype(F32))
        tile = jnp.where(lane == 0, below, jnp.where(lane == 1, own, above))
        tiles[view] = tile
        up[view, C] = tile
        down[view, C] = tile


def shift_rows(offsets, held, low, high, tiles, after, out, marks, main):
    has_low, has_high = edges("by")
    lane = lanes(8)
    for view in range(V):
        main[view, :, 0:OFF] = jnp.where(has_low, low[view, :C], 0.0)
        main[view, :, OFF + C :] = jnp.where(has_high, high[view, :C], 0.0)
        out[view] = main[view, :, pl.ds(OFF + offsets[1, view], C)]
        below = jnp.where(has_low, low[view, C], 0.0)
        above = jnp.where(has_high, high[view, C], 0.0)
        middle = pltpu.roll(tiles[view], 3, 1)
        above = pltpu.roll(above, 6, 1)
        marks[view] = jnp.where(lane < 3, below, jnp.where(lane < 6, middle, above))


def divide(
    offsets, cover, forward_z, blurred, high, low, seen, marks, ratio, near, far
):
    has_low, has_high = edges("bz")
    lane = lanes(1)
    for view in range(V):
        block = blurred[view].reshape(C * C, Z)
        block = jnp.concatenate([block, sides(low[view, :64], high[view, :64])], axis=1)
        model = dot(block, forward_z[view]).reshape(C, C, Z)
        before = jnp.where(even(), high[view, 64:65], low[view, 64:65])
        after = jnp.where(even(), low[view, 64:65], high[view, 64:65])
        before = jnp.where(has_low, before, 0.0)
        after = jnp.where(has_high, after, 0.0)
        own = jnp.full((1, Z), cover[view].astype(F32))
        place = lane - offsets[2, view]
        mask = jnp.where(place < 0, before, jnp.where(place < Z, own, after))
        block = jnp.where(mask > 0.0, mask * seen[view] / model, 0.0)
        ratio[view] = block
        pack_sides(block, near, far, view)
        near[view, 64:] = marks[view]
        far[view, 64:] = marks[view]


def spread(source, taps, planes, row):
    for a in range(1, W - 1):
        total = None
        for i in range(C):
            t = a - i - 1
            if 0 <= t < K:
                term = taps[t] * source[i]
                total = term if total is None else total + term
        planes[a, pl.ds(pl.multiple_of(row, 8), 8), :] = total


def back_own(
    table, fan_out, backward_z, ratio, out_low, out_mid, out_high, planes
):
    @pl.loop(0, V)
    def _(view):
        back = dot(ratio[view].reshape(C * C, Z), backward_z[view, :Z])
        back = back.reshape(C, C, Z)
        taps = [table[view, t] for t in range(K)]
        for half in range(2):
            source = [back[i, 8 * half : 8 * half + 8, :] for i in range(C)]
            spread(source, taps, planes, view * C + 8 * half)

    planes[0] = jnp.zeros((V * C, Z), F32)
    planes[W - 1] = jnp.zeros((V * C, Z), F32)
    for pair in range(W // 2):
        both = jnp.concatenate([planes[2 * pair], planes[2 * pair + 1]], axis=1)
        both = dot(
            fan_out[:, : 2 * V * C], jnp.concatenate(split(both), axis=0), None
        )
        both = both[:W] + both[W:]
        for part in range(2):
            piece = both[:, part * Z : (part + 1) * Z]
            out_low[2 * pair + part] = piece[:C]
            out_mid[2 * pair + part] = piece[C : 2 * C]
            out_high[2 * pair + part] = piece[2 * C :]


def back_rest(
    table, fan_pair, backward_z, far, near, after, out_low, out_mid, out_high, planes
):
    lane = lanes(8)
    half = lanes(W) < 64

    @pl.loop(0, V // 2)
    def _(pair):
        parts = []
        for odd in range(2):
            view = 2 * pair + odd
            block = sides(near[view, :64], far[view, :64])
            block = dot(block, backward_z[view, Z:])
            parts.append(pltpu.roll(block, 32 + 64 * odd, 1).reshape(C, C, Z))
        taps = [
            jnp.where(lane < 64, table[2 * pair, t], table[2 * pair + 1, t])
            for t in range(K)
        ]
        for half in range(2):
            rows = slice(8 * half, 8 * half + 8)
            source = [
                jnp.where(lane < 64, parts[0][i, rows], parts[1][i, rows])
                for i in range(C)
            ]
            spread(source, taps, planes, pair * C + 8 * half)

    planes[0] = jnp.zeros((W, Z), F32)
    planes[W - 1] = jnp.zeros((W, Z), F32)
    def fold(a):
        first, second = planes[a], planes[a + 1]
        turned, other = pltpu.roll(first, 64, 1), pltpu.roll(second, 64, 1)
        even_rows = jnp.where(half, first, other)
        odd_rows = jnp.where(half, turned, second)
        return jnp.concatenate([even_rows, odd_rows], axis=0)

    for quad in range(W // 4):
        both = jnp.concatenate([fold(4 * quad), fold(4 * quad + 2)], axis=1)
        both = dot(
            fan_pair[:, : 2 * V * C], jnp.concatenate(split(both), axis=0), None
        )
        both = both[:W] + both[W:]
        for part in range(2):
            piece = both[:, part * Z : (part + 1) * Z]
            out_low[2 * quad + part] = piece[:C]
            out_mid[2 * quad + part] = piece[C : 2 * C]
            out_high[2 * quad + part] = piece[2 * C :]


def add_rows(
    mid, from_low, from_high, rest, rest_low, rest_high, out_low, out_mid, out_high
):
    has_low, has_high = edges("by")
    lane = lanes(C)
    ends = jnp.logical_or(lane < 32, lane >= 96)
    for a in range(W):
        total = (
            mid[a]
            + jnp.where(has_low, from_low[a], 0.0)
            + jnp.where(has_high, from_high[a], 0.0)
        )
        more = (
            rest[a // 2]
            + jnp.where(has_low, rest_low[a // 2], 0.0)
            + jnp.where(has_high, rest_high[a // 2], 0.0)
        )
        more = pltpu.roll(more, 32 if a % 2 else 96, 1)
        total = total + jnp.where(ends, more, 0.0)
        if a < C:
            out_low[a] = total
        elif a < 2 * C:
            out_mid[a - C] = total
        else:
            out_high[a - 2 * C] = total


def part(tap, cell, count, which):
    before = jnp.where(tap > cell + R, 1.0, 0.0)
    after = jnp.where(tap < cell + R + 1 - count, 1.0, 0.0)
    return jnp.where(which == 0, before, jnp.where(which == 2, after, 1.0 - before - after))


def weigh(norm, marks, near_marks, far_marks, weights):
    has_low, has_high = edges("bz")
    tap = lax.broadcasted_iota(jnp.int32, (Z, Z), 0)
    cell = lax.broadcasted_iota(jnp.int32, (Z, Z), 1)
    part_x = [dot(norm[0], part(tap, cell, C, p), HIGHEST) for p in range(3)]
    part_z = [dot(norm[2], part(tap, cell, Z, r), HIGHEST) for r in range(3)]
    part_y = [dot(norm[1], part(tap, cell, C, q), HIGHEST) for q in range(3)]
    part_y = [jnp.concatenate([y] * C, axis=0).T for y in part_y]
    sums = [jnp.zeros((C, Z), F32) for _ in range(C)]
    for view in range(V):
        low = jnp.where(even(), far_marks[view, 0:1], near_marks[view, 0:1])
        high = jnp.where(even(), near_marks[view, 0:1], far_marks[view, 0:1])
        near = [
            jnp.where(has_low, low, 0.0),
            marks[view, 0:1],
            jnp.where(has_high, high, 0.0),
        ]
        share = [
            jnp.broadcast_to(part_y[q][:C, view : view + 1], (C, Z)) for q in range(3)
        ]
        for p in range(3):
            term = None
            for r in range(3):
                level = None
                for q in range(3):
                    at = 3 * q + p
                    cell = jnp.broadcast_to(near[r][:, at : at + 1], (C, Z)) * share[q]
                    level = cell if level is None else level + cell
                level = level * part_z[r][view : view + 1, :]
                term = level if term is None else term + level
            for i in range(C):
                scale = jnp.broadcast_to(part_x[p][view : view + 1, i : i + 1], (C, Z))
                sums[i] = sums[i] + scale * term
    for i in range(C):
        weights[i] = sums[i]


def finish(estimate, mid, from_low, from_high, weights, out):
    has_low, has_high = edges("bx")
    total = (
        mid[...]
        + jnp.where(has_low, from_low[...], 0.0)
        + jnp.where(has_high, from_high[...], 0.0)
    )
    out[...] = estimate[...] * total / weights[...]


def on_device(estimate, raw, psf, offsets, coverage):
    cover = coverage.reshape(V)
    offsets = offsets.T
    full = (V, C, C, Z)

    left = shift(estimate, "bx", 1)
    right = shift(estimate, "bx", -1)
    up, down = call(
        pack_planes,
        [(V, OFF + 1, C, Z)] * 2,
        [HBM, VM],
        [pltpu.SMEM((V,), jnp.int32), pltpu.SemaphoreType.DMA],
        moved=3 << 19,
    )(cover, raw)
    raw_low = shift(up, "bx", 1)
    raw_high = shift(down, "bx", -1)
    (wide,) = call(
        join_planes,
        [(W, C, Z)],
        [VM, HBM, VM],
        [pltpu.SemaphoreType.DMA],
        moved=1 << 18,
    )(left, estimate, right)
    norm, table, fan_in, fan_out, fan_pair, forward_z, backward_z = call(
        build,
        [
            (3, 8, Z),
            (V, K, 8, Z),
            jax.ShapeDtypeStruct((V * C, 2 * Z), BF16),
            jax.ShapeDtypeStruct((2 * W, 2 * Z), BF16),
            jax.ShapeDtypeStruct((2 * W, 2 * Z), BF16),
            (V, 2 * Z, Z),
            (V, 2 * Z, Z),
        ],
        [SM, VM, ANY],
        moved=1 << 23,
    )(offsets, psf, wide)
    low = shift(wide, "by", 1)
    high = shift(wide, "by", -1)

    shifted, up, down, tiles = call(
        shift_planes,
        [
            (V, C, 2 * C, Z),
            (V, C + 1, OFF, Z),
            (V, C + 1, OFF, Z),
            (V, 8, Z),
        ],
        [SM, SM, VM, VM, VM, ANY],
        [pltpu.VMEM((V, 2 * C, C, Z), F32)],
        moved=1 << 26,
    )(offsets, cover, raw, raw_low, raw_high, norm)
    raw_low = shift(up, "by", 1)
    raw_high = shift(down, "by", -1)

    blurred, near, far = call(
        forward,
        [full, (V, 72, Z), (V, 72, Z)],
        [VM] * 5 + [SM, ANY],
        [pltpu.VMEM((W, V * C, Z), F32)],
        flops=1 << 34,
        moved=1 << 26,
    )(table, fan_in, wide, low, high, cover, tiles)
    far, near = swap(far, 1), swap(near, 0)

    seen, marks, _ = call(
        shift_rows,
        [full, (V, 8, Z), (V, C, 2 * C, Z)],
        [SM] + [VM] * 4 + [ANY],
        alias={1: 2},
        moved=1 << 26,
    )(offsets, shifted, raw_low, raw_high, tiles, blurred)

    ratio, near, far = call(
        divide,
        [full, (V, 72, Z), (V, 72, Z)],
        [SM, SM] + [VM] * 6,
        flops=1 << 34,
        moved=1 << 26,
    )(offsets, cover, forward_z, blurred, far, near, seen, marks)
    far, near = swap(far, 1), swap(near, 0)

    out_low, out_mid, out_high = call(
        back_own,
        [(W, C, Z)] * 3,
        [VM] * 4,
        [pltpu.VMEM((W, V * C, Z), F32)],
        flops=1 << 34,
        moved=1 << 26,
    )(table, fan_out, backward_z, ratio)
    sum_low = shift(out_high, "by", 1)
    sum_high = shift(out_low, "by", -1)
    rest_low, rest_mid, rest_high = call(
        back_rest,
        [(W // 2, C, Z)] * 3,
        [VM] * 5 + [ANY],
        [pltpu.VMEM((W, W, Z), F32)],
        flops=1 << 34,
        moved=1 << 26,
    )(table, fan_pair, backward_z, far, near, out_mid)
    more_low = shift(rest_high, "by", 1)
    more_high = shift(rest_low, "by", -1)
    last = pl.BlockSpec((V, 8, Z), lambda i: (0, 8, 0))
    (weights,) = call(
        weigh, [(C, C, Z)], [VM, VM, last, last], grid=(1,), moved=1 << 19
    )(norm, marks, near, far)
    out_low, out_mid, out_high = call(
        add_rows, [(C, C, Z)] * 3, [VM] * 6, moved=3 << 19
    )(out_mid, sum_low, sum_high, rest_mid, more_low, more_high)
    sum_low = shift(out_high, "bx", 1)
    sum_high = shift(out_low, "bx", -1)
    (out,) = call(finish, [(C, C, Z)], [VM] * 5, moved=3 << 18)(
        estimate, out_mid, sum_low, sum_high, weights
    )
    return out


def solution(mesh):
    return jax.shard_map(
        on_device,
        mesh=mesh,
        in_specs=(
            P("bx", "by", "bz"),
            P(None, "bx", "by", "bz"),
            P(),
            P(),
            P(None, "bx", "by", "bz"),
        ),
        out_specs=P("bx", "by", "bz"),
        check_vma=False,
    )
```

```python
import jax
import jax.numpy as jnp
from jax import lax
from jax.experimental import pallas as pl
from jax.experimental.pallas import tpu as pltpu
from jax.sharding import PartitionSpec as P

V = 6
K = 31
R = 15
OFF = 8
C = 16
Z = 128
W = 3 * C
N = W - 2
HIGH = lax.Precision.HIGH
HIGHEST = lax.Precision.HIGHEST
F32 = jnp.float32
BF16 = jnp.bfloat16

VM = pl.BlockSpec(memory_space=pltpu.VMEM)
SM = pl.BlockSpec(memory_space=pltpu.SMEM)
ANY = pl.BlockSpec(memory_space=pl.ANY)
HBM = pl.BlockSpec(memory_space=pltpu.HBM)


def call(
    body, outs, specs, scratch=(), out_specs=None, grid=(), alias=None,
    flops=0, moved=0, vmem=16,
):
    return pl.pallas_call(
        body,
        grid=grid,
        out_shape=[
            s if hasattr(s, "dtype") else jax.ShapeDtypeStruct(s, F32) for s in outs
        ],
        in_specs=specs,
        out_specs=out_specs or [VM] * len(outs),
        scratch_shapes=list(scratch),
        input_output_aliases=alias or {},
        compiler_params=pltpu.CompilerParams(vmem_limit_bytes=vmem << 20),
        cost_estimate=pl.CostEstimate(
            flops=flops, bytes_accessed=moved, transcendentals=0
        ),
    )


def edges(axis):
    place = lax.axis_index(axis)
    return place > 0, place < lax.axis_size(axis) - 1


def even(axis="bz"):
    return lax.rem(lax.axis_index(axis), 2) == 0


def choose(axis, first, second):
    has_low, has_high = edges(axis)
    low = jnp.where(even(axis), second, first)
    high = jnp.where(even(axis), first, second)
    return jnp.where(has_low, low, 0.0), jnp.where(has_high, high, 0.0)


def trade(block, axis, first):
    count, depth = lax.axis_size(axis), lax.axis_size("bz")
    pairs = []
    for i in range(count):
        j = i + 1 if (i - first) % 2 == 0 else i - 1
        for z in range(depth):
            target = j * depth + z if 0 <= j < count else i * depth + (z ^ 1)
            pairs.append((i * depth + z, target))
    return lax.ppermute(block, (axis, "bz"), pairs)


def swap(block, first):
    count = lax.axis_size("bz")
    pairs = []
    for i in range(first, count, 2):
        a, b = i % count, (i + 1) % count
        pairs += [(a, b), (b, a)]
    return lax.ppermute(block, "bz", pairs)


def lanes(rows):
    return lax.broadcasted_iota(jnp.int32, (rows, Z), 1)


def dot(a, b, precision=HIGH):
    return jnp.dot(a, b, precision=precision, preferred_element_type=F32)


def split(block):
    high = block.astype(BF16)
    return high, (block - high.astype(F32)).astype(BF16)


def pack_planes(cover, own, raw, held, up, down, flags, sem):
    tag = pltpu.make_async_copy(cover, flags, sem)
    tag.start()
    held[C - 1 : 2 * C - 1] = own[...]
    for view in range(V):
        at = slice(view * OFF, (view + 1) * OFF)
        up[at] = jnp.where(even("bx"), raw[view, OFF:], raw[view, :OFF])
        down[at] = jnp.where(even("bx"), raw[view, :OFF], raw[view, OFF:])
    tag.wait()
    for view in range(V):
        tile = jnp.full((1, Z), flags[view].astype(F32))
        up[V * OFF, view : view + 1] = tile
        down[V * OFF, view : view + 1] = tile


def build(
    offsets, psf, after, norm, table, fan_in, fan_out, fan_pair,
    forward_z, backward_z,
):
    norm[...] = jnp.zeros((3, 8, Z), F32)
    for view in range(V):
        for axis in range(3):
            line = psf[view, axis : axis + 1, :]
            norm[axis, view : view + 1, 0:K] = line / jnp.sum(
                line, axis=1, keepdims=True
            )
    bands = []
    for view in range(V):
        line = norm[0, view : view + 1, :]
        for t in range(K):
            table[view, t] = jnp.broadcast_to(line[:, t : t + 1], (8, Z))
        row = jnp.broadcast_to(norm[1, view : view + 1, :], (C, Z))
        bands.append(pltpu.roll(row, 1, 1, stride=1, stride_axis=0))
        row = norm[2, view : view + 1, :]
        row = jnp.concatenate([row, jnp.zeros((1, Z), F32)], axis=1)
        row = jnp.broadcast_to(row, (2 * Z, 2 * Z))
        band = pltpu.roll(row, 2 * Z - R, 1, stride=1, stride_axis=0)
        band = pltpu.roll(band, lax.rem(2 * Z - offsets[2, view], 2 * Z), 1)
        backward_z[view] = band[:, :Z]
        forward_z[view] = band[:Z, :].T
    def side_by_side(*parts):
        total = None
        for turn, block in parts:
            block = block.astype(F32)
            block = jnp.concatenate([block, jnp.zeros_like(block)], axis=1)
            block = pltpu.roll(block, turn, 1) if turn else block
            total = block if total is None else total + block
        return total.astype(BF16)

    high, low = split(jnp.concatenate(bands, axis=0))
    fan_in[...] = side_by_side((0, high), (W, high), (2 * W, low))
    for out, order in ((fan_out, range(V)), (fan_pair, (0, 2, 4, 1, 3, 5))):
        rows = [bands[v] for v in order]
        rows += [jnp.zeros((Z - V * C, Z), F32)]
        high, low = split(jnp.concatenate(rows, axis=0).T[:W, :])
        out[0:W] = side_by_side((0, high), (V * C, high))
        out[W:] = side_by_side((0, low), (V * C, low))


def join_planes(held, low, high, wide):
    low, high = choose("bx", low[...], high[...])
    wide[: C - 1] = low[1:]
    wide[2 * C - 1 :] = high[: C - 1]


def pack_lanes(block, first):
    lane = lanes(64)
    packed = None
    for group in range(4):
        piece = block[4 * group : 4 * group + 4].reshape(64, Z)
        turn = (32 * group - first) % Z
        if turn:
            piece = pltpu.roll(piece, turn, 1)
        packed = piece if packed is None else jnp.where(lane >= 32 * group, piece, packed)
    return packed


def pack_sides(block, near, far, view):
    up = pack_lanes(block, 96)
    down = pack_lanes(block, 0)
    rows = pl.ds(pl.multiple_of(view * 64, 64), 64)
    near[rows, :] = jnp.where(even(), up, down)
    far[rows, :] = jnp.where(even(), down, up)


def forward(table, fan_in, own, low, high, cover, after, blurred, near, far, planes):
    fan = fan_in[:, : 3 * W]
    for pair in range(N // 2):
        sides = []
        for a in (2 * pair, 2 * pair + 1):
            below, above = choose("by", low[a], high[a])
            sides.append(jnp.concatenate([below, own[a], above], axis=0))
        top, rest = split(jnp.concatenate(sides, axis=1))
        both = dot(fan, jnp.concatenate([top, rest, top], axis=0), None)
        planes[2 * pair] = both[:, :Z]
        planes[2 * pair + 1] = both[:, Z:]

    @pl.loop(0, V)
    def _(view):
        taps = [table[view, t] for t in range(K)]
        for half in range(2):
            sums = [None] * C
            for a in range(N):
                plane = planes[a, pl.ds(pl.multiple_of(view * C + 8 * half, 8), 8), :]
                for i in range(C):
                    t = a - i
                    if 0 <= t < K:
                        term = taps[t] * plane
                        sums[i] = term if sums[i] is None else sums[i] + term
            for i in range(C):
                blurred[view, i, 8 * half : 8 * half + 8, :] = sums[i]
        pack_sides(blurred[view], near, far, view)

    for view in range(V):
        tile = jnp.full((1, Z), cover[view].astype(F32))
        near[64 * V + view : 64 * V + view + 1] = tile
        far[64 * V + view : 64 * V + view + 1] = tile


def sides(near, far, view):
    has_low, has_high = edges("bz")
    lane = lanes(64)
    rows = pl.ds(pl.multiple_of(view * 64, 64), 64)
    near, far = near[rows, :], far[rows, :]
    low = jnp.where(even(), far, near)
    high = jnp.where(even(), near, far)
    parts = []
    for group in range(4):
        before = pltpu.roll(low, 96 - 32 * group, 1) if group < 3 else low
        after = pltpu.roll(high, (Z - 32 * group) % Z, 1) if group else high
        before = jnp.where(jnp.logical_and(lane >= 96, has_low), before, 0.0)
        after = jnp.where(jnp.logical_and(lane < 32, has_high), after, 0.0)
        parts.append(before + after)
    return jnp.concatenate(parts, axis=0)


def shift_planes(
    offsets, cover, raw, low, high, after, shifted, up, down, tiles, wide
):
    lane = lanes(8)
    row = lax.broadcasted_iota(jnp.int32, (8, Z), 0)
    own = jnp.zeros((8, Z), F32)
    for view in range(V):
        at = slice(view * OFF, (view + 1) * OFF)
        below, above = choose("bx", low[at], high[at])
        wide[view, 0:OFF] = below
        wide[view, OFF : OFF + C] = raw[view]
        wide[view, OFF + C :] = above
        block = wide[view, pl.ds(OFF + offsets[0, view], C)]
        shifted[view, :, OFF : OFF + C] = block
        at = slice(view * C, (view + 1) * C)
        up[at] = jnp.where(even("by"), block[:, OFF:], block[:, :OFF])
        down[at] = jnp.where(even("by"), block[:, :OFF], block[:, OFF:])
        own = jnp.where(row == view, cover[view].astype(F32), own)
    below, above = choose("bx", low[V * OFF, 0:8], high[V * OFF, 0:8])
    tile = jnp.where(lane == 0, below, jnp.where(lane == 1, own, above))
    tiles[...] = tile
    up[V * C] = tile
    down[V * C] = tile


def shift_rows(offsets, held, low, high, tiles, after, out, marks, main):
    lane = lanes(8)
    for view in range(V):
        at = slice(view * C, (view + 1) * C)
        below, above = choose("by", low[at], high[at])
        main[view, :, 0:OFF] = below
        main[view, :, OFF + C :] = above
        out[view] = main[view, :, pl.ds(OFF + offsets[1, view], C)]
    below, above = choose("by", low[V * C], high[V * C])
    middle = pltpu.roll(tiles[...], 3, 1)
    above = pltpu.roll(above, 6, 1)
    marks[...] = jnp.where(lane < 3, below, jnp.where(lane < 6, middle, above))


def model_own(forward_z, blurred, after, out):
    for view in range(V):
        block = dot(blurred[view].reshape(C * C, Z), forward_z[view, :Z])
        out[view] = block.reshape(C, C, Z)


def divide(
    offsets, cover, forward_z, model, high, low, seen, marks, ratio, near, far
):
    has_low, has_high = edges("bz")
    lane = lanes(1)
    for view in range(V):
        block = dot(sides(low, high, view), forward_z[view, Z:])
        block = model[view] + block.reshape(C, C, Z)
        at = slice(64 * V + view, 64 * V + view + 1)
        before = jnp.where(even(), high[at], low[at])
        after = jnp.where(even(), low[at], high[at])
        before = jnp.where(has_low, before, 0.0)
        after = jnp.where(has_high, after, 0.0)
        own = jnp.full((1, Z), cover[view].astype(F32))
        place = lane - offsets[2, view]
        mask = jnp.where(place < 0, before, jnp.where(place < Z, own, after))
        block = jnp.where(mask > 0.0, mask * seen[view] / block, 0.0)
        ratio[view] = block
        pack_sides(block, near, far, view)
    near[64 * V :] = marks[...]
    far[64 * V :] = marks[...]


def spread(source, taps, planes, row):
    for a in range(N):
        total = None
        for i in range(C):
            t = a - i
            if 0 <= t < K:
                term = taps[t] * source[i]
                total = term if total is None else total + term
        planes[a, pl.ds(pl.multiple_of(row, 8), 8), :] = total


def put(at, piece, first, mid, second):
    mid[at] = piece[C : 2 * C]
    first[at] = jnp.where(even("by"), piece[2 * C :], piece[:C])
    second[at] = jnp.where(even("by"), piece[:C], piece[2 * C :])


def back_own(
    table, fan_out, backward_z, ratio, first, out_mid, second, planes
):
    @pl.loop(0, V)
    def _(view):
        back = dot(ratio[view].reshape(C * C, Z), backward_z[view, :Z])
        back = back.reshape(C, C, Z)
        taps = [table[view, t] for t in range(K)]
        for half in range(2):
            source = [back[i, 8 * half : 8 * half + 8, :] for i in range(C)]
            spread(source, taps, planes, view * C + 8 * half)

    for pair in range(N // 2):
        both = jnp.concatenate([planes[2 * pair], planes[2 * pair + 1]], axis=1)
        both = dot(
            fan_out[:, : 2 * V * C], jnp.concatenate(split(both), axis=0), None
        )
        both = both[:W] + both[W:]
        for part in range(2):
            piece = both[:, part * Z : (part + 1) * Z]
            put(2 * pair + part, piece, first, out_mid, second)


def back_rest(
    table, fan_pair, backward_z, far, near, after, out_first, out_mid, out_second, planes
):
    lane = lanes(8)
    half = lanes(W) < 64

    @pl.loop(0, V // 2)
    def _(pair):
        parts = []
        for odd in range(2):
            view = 2 * pair + odd
            block = sides(near, far, view)
            block = dot(block, backward_z[view, Z:])
            parts.append(pltpu.roll(block, 32 + 64 * odd, 1).reshape(C, C, Z))
        taps = [
            jnp.where(lane < 64, table[2 * pair, t], table[2 * pair + 1, t])
            for t in range(K)
        ]
        for half in range(2):
            rows = slice(8 * half, 8 * half + 8)
            source = [
                jnp.where(lane < 64, parts[0][i, rows], parts[1][i, rows])
                for i in range(C)
            ]
            spread(source, taps, planes, pair * C + 8 * half)

    planes[N] = jnp.zeros((W, Z), F32)
    planes[N + 1] = jnp.zeros((W, Z), F32)

    def fold(a):
        first, second = planes[a], planes[a + 1]
        turned, other = pltpu.roll(first, 64, 1), pltpu.roll(second, 64, 1)
        even_rows = jnp.where(half, first, other)
        odd_rows = jnp.where(half, turned, second)
        return jnp.concatenate([even_rows, odd_rows], axis=0)

    for quad in range(W // 4):
        both = jnp.concatenate([fold(4 * quad), fold(4 * quad + 2)], axis=1)
        both = dot(
            fan_pair[:, : 2 * V * C], jnp.concatenate(split(both), axis=0), None
        )
        both = both[:W] + both[W:]
        for part in range(min(2, N // 2 - 2 * quad)):
            piece = both[:, part * Z : (part + 1) * Z]
            put(2 * quad + part, piece, out_first, out_mid, out_second)


def add_rows(
    mid, from_low, from_high, rest, rest_low, rest_high, out_mid, first, second,
    out_low, out_high,
):
    lane = lanes(C)
    ends = jnp.logical_or(lane < 32, lane >= 96)
    out_low[0] = jnp.zeros((C, Z), F32)
    out_high[C - 1] = jnp.zeros((C, Z), F32)
    for a in range(N):
        below, above = choose("by", from_low[a], from_high[a])
        total = mid[a] + below + above
        below, above = choose("by", rest_low[a // 2], rest_high[a // 2])
        more = rest[a // 2] + below + above
        more = pltpu.roll(more, 32 if a % 2 else 96, 1)
        total = total + jnp.where(ends, more, 0.0)
        out = (out_low, out_mid, out_high)[(a + 1) // C]
        out[(a + 1) % C] = total
    first[...] = jnp.where(even("bx"), out_high[...], out_low[...])
    second[...] = jnp.where(even("bx"), out_low[...], out_high[...])


def part(tap, cell, count, which):
    before = jnp.where(tap > cell + R, 1.0, 0.0)
    after = jnp.where(tap < cell + R + 1 - count, 1.0, 0.0)
    return jnp.where(which == 0, before, jnp.where(which == 2, after, 1.0 - before - after))


def weigh(norm, estimate, marks, near_marks, far_marks, scale):
    has_low, has_high = edges("bz")
    tap = lax.broadcasted_iota(jnp.int32, (Z, Z), 0)
    cell = lax.broadcasted_iota(jnp.int32, (Z, Z), 1)
    part_x = [dot(norm[0], part(tap, cell, C, p), HIGHEST) for p in range(3)]
    part_z = [dot(norm[2], part(tap, cell, Z, r), HIGHEST) for r in range(3)]
    part_y = [dot(norm[1], part(tap, cell, C, q), HIGHEST) for q in range(3)]
    part_y = [jnp.concatenate([y] * C, axis=0).T for y in part_y]
    sums = [jnp.zeros((C, Z), F32) for _ in range(C)]
    for view in range(V):
        at = slice(view, view + 1)
        low = jnp.where(even(), far_marks[at], near_marks[at])
        high = jnp.where(even(), near_marks[at], far_marks[at])
        near = [
            jnp.where(has_low, low, 0.0),
            marks[at],
            jnp.where(has_high, high, 0.0),
        ]
        share = [
            jnp.broadcast_to(part_y[q][:C, view : view + 1], (C, Z)) for q in range(3)
        ]
        for p in range(3):
            term = None
            for r in range(3):
                level = None
                for q in range(3):
                    at = 3 * q + p
                    cell = jnp.broadcast_to(near[r][:, at : at + 1], (C, Z)) * share[q]
                    level = cell if level is None else level + cell
                level = level * part_z[r][view : view + 1, :]
                term = level if term is None else term + level
            for i in range(C):
                factor = jnp.broadcast_to(part_x[p][view : view + 1, i : i + 1], (C, Z))
                sums[i] = sums[i] + factor * term
    for i in range(C):
        scale[i] = estimate[i] / sums[i]


def finish(scale, mid, from_low, from_high, out):
    low, high = choose("bx", from_low[...], from_high[...])
    total = mid[...] + low + high
    out[...] = scale[...] * total


def on_device(estimate, raw, psf, offsets, coverage):
    cover = coverage.reshape(V)
    offsets = offsets.T
    full = (V, C, C, Z)

    left = trade(estimate, "bx", 0)
    right = trade(estimate, "bx", 1)
    held, up, down = call(
        pack_planes,
        [(N, C, Z)] + [(V * OFF + 1, C, Z)] * 2,
        [HBM, VM, VM],
        [pltpu.SMEM((V,), jnp.int32), pltpu.SemaphoreType.DMA],
        moved=3 << 19,
    )(cover, estimate, raw)
    raw_low = trade(up, "bx", 0)
    raw_high = trade(down, "bx", 1)
    (wide,) = call(join_planes, [(N, C, Z)], [VM] * 3, alias={0: 0}, moved=1 << 18)(
        held, left, right
    )
    norm, table, fan_in, fan_out, fan_pair, forward_z, backward_z = call(
        build,
        [
            (3, 8, Z),
            (V, K, 8, Z),
            jax.ShapeDtypeStruct((V * C, 2 * Z), BF16),
            jax.ShapeDtypeStruct((2 * W, 2 * Z), BF16),
            jax.ShapeDtypeStruct((2 * W, 2 * Z), BF16),
            (V, 2 * Z, Z),
            (V, 2 * Z, Z),
        ],
        [SM, VM, ANY],
        moved=1 << 23,
    )(offsets, psf, wide)
    low = trade(wide, "by", 0)
    high = trade(wide, "by", 1)

    shifted, up, down, tiles = call(
        shift_planes,
        [
            (V, C, 2 * C, Z),
            (V * C + 1, OFF, Z),
            (V * C + 1, OFF, Z),
            (8, Z),
        ],
        [SM, SM, VM, VM, VM, ANY],
        [pltpu.VMEM((V, 2 * C, C, Z), F32)],
        moved=1 << 26,
    )(offsets, cover, raw, raw_low, raw_high, norm)
    raw_low = trade(up, "by", 0)
    raw_high = trade(down, "by", 1)

    blurred, near, far = call(
        forward,
        [full, (64 * V + 8, Z), (64 * V + 8, Z)],
        [VM] * 5 + [SM, ANY],
        [pltpu.VMEM((N, V * C, Z), F32)],
        flops=1 << 34,
        moved=1 << 26,
    )(table, fan_in, wide, low, high, cover, tiles)
    far, near = swap(far, 1), swap(near, 0)

    seen, marks, _ = call(
        shift_rows,
        [full, (8, Z), (V, C, 2 * C, Z)],
        [SM] + [VM] * 4 + [ANY],
        alias={1: 2},
        moved=1 << 26,
    )(offsets, shifted, raw_low, raw_high, tiles, blurred)

    (model,) = call(
        model_own, [full], [VM, VM, ANY], flops=1 << 30, moved=3 << 20
    )(forward_z, blurred, seen)
    ratio, near, far = call(
        divide,
        [full, (64 * V + 8, Z), (64 * V + 8, Z)],
        [SM, SM] + [VM] * 6,
        flops=1 << 34,
        moved=1 << 26,
    )(offsets, cover, forward_z, model, far, near, seen, marks)
    far, near = swap(far, 1), swap(near, 0)

    first, out_mid, second = call(
        back_own,
        [(N, C, Z)] * 3,
        [VM] * 4,
        [pltpu.VMEM((N, V * C, Z), F32)],
        flops=1 << 34,
        moved=1 << 26,
    )(table, fan_out, backward_z, ratio)
    sum_low = trade(first, "by", 0)
    sum_high = trade(second, "by", 1)
    rest_first, rest_mid, rest_second = call(
        back_rest,
        [(N // 2, C, Z)] * 3,
        [VM] * 5 + [ANY],
        [pltpu.VMEM((W, W, Z), F32)],
        flops=1 << 34,
        moved=1 << 26,
    )(table, fan_pair, backward_z, far, near, out_mid)
    more_low = trade(rest_first, "by", 0)
    more_high = trade(rest_second, "by", 1)
    last = pl.BlockSpec((8, Z), lambda i: (8 * V, 0))
    (scale,) = call(
        weigh, [(C, C, Z)], [VM, VM, VM, last, last], grid=(1,), moved=1 << 19
    )(norm, estimate, marks, near, far)
    out_mid, first, second = call(
        add_rows,
        [(C, C, Z)] * 3,
        [VM] * 6,
        [pltpu.VMEM((C, C, Z), F32)] * 2,
        moved=3 << 19,
    )(out_mid, sum_low, sum_high, rest_mid, more_low, more_high)
    sum_low = trade(first, "bx", 0)
    sum_high = trade(second, "bx", 1)
    (out,) = call(finish, [(C, C, Z)], [VM] * 4, moved=3 << 18)(
        scale, out_mid, sum_low, sum_high
    )
    return out


def solution(mesh):
    return jax.shard_map(
        on_device,
        mesh=mesh,
        in_specs=(
            P("bx", "by", "bz"),
            P(None, "bx", "by", "bz"),
            P(),
            P(),
            P(None, "bx", "by", "bz"),
        ),
        out_specs=P("bx", "by", "bz"),
        check_vma=False,
    )
```

```python
import jax
import jax.numpy as jnp
from jax import lax
from jax.experimental import pallas as pl
from jax.experimental.pallas import tpu as pltpu
from jax.sharding import PartitionSpec as P

V = 6
K = 31
R = 15
OFF = 8
C = 16
Z = 128
W = 3 * C
N = W - 2
HIGH = lax.Precision.HIGH
HIGHEST = lax.Precision.HIGHEST
F32 = jnp.float32
BF16 = jnp.bfloat16

VM = pl.BlockSpec(memory_space=pltpu.VMEM)
SM = pl.BlockSpec(memory_space=pltpu.SMEM)
ANY = pl.BlockSpec(memory_space=pl.ANY)
HBM = pl.BlockSpec(memory_space=pltpu.HBM)


def call(
    body, outs, specs, scratch=(), out_specs=None, grid=(), alias=None,
    flops=0, moved=0, vmem=16,
):
    return pl.pallas_call(
        body,
        grid=grid,
        out_shape=[
            s if hasattr(s, "dtype") else jax.ShapeDtypeStruct(s, F32) for s in outs
        ],
        in_specs=specs,
        out_specs=out_specs or [VM] * len(outs),
        scratch_shapes=list(scratch),
        input_output_aliases=alias or {},
        compiler_params=pltpu.CompilerParams(vmem_limit_bytes=vmem << 20),
        cost_estimate=pl.CostEstimate(
            flops=flops, bytes_accessed=moved, transcendentals=0
        ),
    )


def edges(axis):
    place = lax.axis_index(axis)
    return place > 0, place < lax.axis_size(axis) - 1


def even(axis="bz"):
    return lax.rem(lax.axis_index(axis), 2) == 0


def choose(axis, first, second):
    has_low, has_high = edges(axis)
    low = jnp.where(even(axis), second, first)
    high = jnp.where(even(axis), first, second)
    return jnp.where(has_low, low, 0.0), jnp.where(has_high, high, 0.0)


def trade(block, axis, first):
    count, depth = lax.axis_size(axis), lax.axis_size("bz")
    pairs = []
    for i in range(count):
        j = i + 1 if (i - first) % 2 == 0 else i - 1
        for z in range(depth):
            target = j * depth + z if 0 <= j < count else i * depth + (z ^ 1)
            pairs.append((i * depth + z, target))
    return lax.ppermute(block, (axis, "bz"), pairs)


def swap(block, first):
    count = lax.axis_size("bz")
    pairs = []
    for i in range(first, count, 2):
        a, b = i % count, (i + 1) % count
        pairs += [(a, b), (b, a)]
    return lax.ppermute(block, "bz", pairs)


def lanes(rows):
    return lax.broadcasted_iota(jnp.int32, (rows, Z), 1)


def dot(a, b, precision=HIGH):
    return jnp.dot(a, b, precision=precision, preferred_element_type=F32)


def split(block):
    high = block.astype(BF16)
    return high, (block - high.astype(F32)).astype(BF16)


def pack_planes(cover, raw, up, down, flags, sem):
    tag = pltpu.make_async_copy(cover, flags, sem)
    tag.start()
    for view in range(V):
        at = slice(view * OFF, (view + 1) * OFF)
        up[at] = jnp.where(even("bx"), raw[view, OFF:], raw[view, :OFF])
        down[at] = jnp.where(even("bx"), raw[view, :OFF], raw[view, OFF:])
    tag.wait()
    for view in range(V):
        tile = jnp.full((1, Z), flags[view].astype(F32))
        up[V * OFF, view : view + 1] = tile
        down[V * OFF, view : view + 1] = tile


def build(
    offsets, psf, after, norm, table, fan_in, fan_out, fan_pair,
    forward_z, backward_z, rest_z,
):
    norm[...] = jnp.zeros((3, 8, Z), F32)
    for view in range(V):
        for axis in range(3):
            line = psf[view, axis : axis + 1, :]
            norm[axis, view : view + 1, 0:K] = line / jnp.sum(
                line, axis=1, keepdims=True
            )
    bands = []
    for view in range(V):
        line = norm[0, view : view + 1, :]
        for t in range(K):
            table[view, t] = jnp.broadcast_to(line[:, t : t + 1], (8, Z))
        row = jnp.broadcast_to(norm[1, view : view + 1, :], (C, Z))
        bands.append(pltpu.roll(row, 1, 1, stride=1, stride_axis=0))
        row = norm[2, view : view + 1, :]
        row = jnp.concatenate([row, jnp.zeros((1, Z), F32)], axis=1)
        row = jnp.broadcast_to(row, (2 * Z, 2 * Z))
        band = pltpu.roll(row, 2 * Z - R, 1, stride=1, stride_axis=0)
        band = pltpu.roll(band, lax.rem(2 * Z - offsets[2, view], 2 * Z), 1)
        backward_z[view] = band[:Z, :Z]
        rest_z[view] = pltpu.roll(band[Z:, :Z], 32 + 64 * (view % 2), 1)
        forward_z[view] = band[:Z, :].T
    def side_by_side(*parts):
        total = None
        for turn, block in parts:
            block = block.astype(F32)
            block = jnp.concatenate([block, jnp.zeros_like(block)], axis=1)
            block = pltpu.roll(block, turn, 1) if turn else block
            total = block if total is None else total + block
        return total.astype(BF16)

    high, low = split(jnp.concatenate(bands, axis=0))
    fan_in[...] = side_by_side((0, high), (W, high), (2 * W, low))
    for out, order in ((fan_out, range(V)), (fan_pair, (0, 2, 4, 1, 3, 5))):
        rows = [bands[v] for v in order]
        rows += [jnp.zeros((Z - V * C, Z), F32)]
        high, low = split(jnp.concatenate(rows, axis=0).T[:W, :])
        out[0:W] = side_by_side((0, high), (V * C, high))
        out[W:] = side_by_side((0, low), (V * C, low))


def join_planes(own, low, high, wide, sem):
    copy = pltpu.make_async_copy(own, wide.at[pl.ds(C - 1, C)], sem)
    copy.start()
    low, high = choose("bx", low[...], high[...])
    wide[: C - 1] = low[1:]
    wide[2 * C - 1 :] = high[: C - 1]
    copy.wait()


def pack_lanes(block, first):
    lane = lanes(64)
    packed = None
    for group in range(4):
        piece = block[4 * group : 4 * group + 4].reshape(64, Z)
        turn = (32 * group - first) % Z
        if turn:
            piece = pltpu.roll(piece, turn, 1)
        packed = piece if packed is None else jnp.where(lane >= 32 * group, piece, packed)
    return packed


def pack_sides(block, near, far, view):
    up = pack_lanes(block, 96)
    down = pack_lanes(block, 0)
    rows = pl.ds(pl.multiple_of(view * 64, 64), 64)
    near[rows, :] = jnp.where(even(), up, down)
    far[rows, :] = jnp.where(even(), down, up)


def forward(table, fan_in, own, low, high, cover, after, blurred, near, far, planes):
    fan = fan_in[:, : 3 * W]
    for pair in range(N // 2):
        sides = []
        for a in (2 * pair, 2 * pair + 1):
            below, above = choose("by", low[a], high[a])
            sides.append(jnp.concatenate([below, own[a], above], axis=0))
        top, rest = split(jnp.concatenate(sides, axis=1))
        both = dot(fan, jnp.concatenate([top, rest, top], axis=0), None)
        planes[2 * pair] = both[:, :Z]
        planes[2 * pair + 1] = both[:, Z:]

    for view in range(V):
        taps = [table[view, t] for t in range(K)]
        for half in range(2):
            sums = [None] * C
            for a in range(N):
                plane = planes[a, pl.ds(pl.multiple_of(view * C + 8 * half, 8), 8), :]
                for i in range(C):
                    t = a - i
                    if 0 <= t < K:
                        term = taps[t] * plane
                        sums[i] = term if sums[i] is None else sums[i] + term
            for i in range(C):
                blurred[view, i, 8 * half : 8 * half + 8, :] = sums[i]
        pack_sides(blurred[view], near, far, view)

    for view in range(V):
        tile = jnp.full((1, Z), cover[view].astype(F32))
        near[64 * V + view : 64 * V + view + 1] = tile
        far[64 * V + view : 64 * V + view + 1] = tile


def sides(near, far, view):
    has_low, has_high = edges("bz")
    lane = lanes(64)
    rows = pl.ds(pl.multiple_of(view * 64, 64), 64)
    near, far = near[rows, :], far[rows, :]
    low = jnp.where(even(), far, near)
    high = jnp.where(even(), near, far)
    parts = []
    for group in range(4):
        before = pltpu.roll(low, 96 - 32 * group, 1) if group < 3 else low
        after = pltpu.roll(high, (Z - 32 * group) % Z, 1) if group else high
        before = jnp.where(jnp.logical_and(lane >= 96, has_low), before, 0.0)
        after = jnp.where(jnp.logical_and(lane < 32, has_high), after, 0.0)
        parts.append(before + after)
    return jnp.concatenate(parts, axis=0)


def shift_planes(
    offsets, cover, raw, low, high, after, shifted, up, down, tiles, wide
):
    lane = lanes(8)
    row = lax.broadcasted_iota(jnp.int32, (8, Z), 0)
    own = jnp.zeros((8, Z), F32)
    for view in range(V):
        at = slice(view * OFF, (view + 1) * OFF)
        below, above = choose("bx", low[at], high[at])
        wide[view, 0:OFF] = below
        wide[view, OFF : OFF + C] = raw[view]
        wide[view, OFF + C :] = above
        block = wide[view, pl.ds(OFF + offsets[0, view], C)]
        shifted[view, :, OFF : OFF + C] = block
        at = slice(view * C, (view + 1) * C)
        up[at] = jnp.where(even("by"), block[:, OFF:], block[:, :OFF])
        down[at] = jnp.where(even("by"), block[:, :OFF], block[:, OFF:])
        own = jnp.where(row == view, cover[view].astype(F32), own)
    below, above = choose("bx", low[V * OFF, 0:8], high[V * OFF, 0:8])
    tile = jnp.where(lane == 0, below, jnp.where(lane == 1, own, above))
    tiles[...] = tile
    up[V * C] = tile
    down[V * C] = tile


def shift_rows(offsets, held, low, high, tiles, after, out, marks, main):
    lane = lanes(8)
    for view in range(V):
        at = slice(view * C, (view + 1) * C)
        below, above = choose("by", low[at], high[at])
        main[view, :, 0:OFF] = below
        main[view, :, OFF + C :] = above
        out[view] = main[view, :, pl.ds(OFF + offsets[1, view], C)]
    below, above = choose("by", low[V * C], high[V * C])
    middle = pltpu.roll(tiles[...], 3, 1)
    above = pltpu.roll(above, 6, 1)
    marks[...] = jnp.where(lane < 3, below, jnp.where(lane < 6, middle, above))


def model_own(forward_z, blurred, after, out):
    for view in range(V):
        block = dot(blurred[view].reshape(C * C, Z), forward_z[view, :Z])
        out[view] = block.reshape(C, C, Z)


def divide(
    offsets, cover, forward_z, model, high, low, seen, marks, ratio, near, far
):
    has_low, has_high = edges("bz")
    lane = lanes(1)
    for view in range(V):
        block = dot(sides(low, high, view), forward_z[view, Z:])
        block = model[view] + block.reshape(C, C, Z)
        at = slice(64 * V + view, 64 * V + view + 1)
        before = jnp.where(even(), high[at], low[at])
        after = jnp.where(even(), low[at], high[at])
        before = jnp.where(has_low, before, 0.0)
        after = jnp.where(has_high, after, 0.0)
        own = jnp.full((1, Z), cover[view].astype(F32))
        place = lane - offsets[2, view]
        mask = jnp.where(place < 0, before, jnp.where(place < Z, own, after))
        block = jnp.where(mask > 0.0, mask * seen[view] / block, 0.0)
        ratio[view] = block
        pack_sides(block, near, far, view)
    near[64 * V :] = marks[...]
    far[64 * V :] = marks[...]


def spread(source, taps, planes, row):
    for a in range(N):
        total = None
        for i in range(C):
            t = a - i
            if 0 <= t < K:
                term = taps[t] * source[i]
                total = term if total is None else total + term
        planes[a, pl.ds(pl.multiple_of(row, 8), 8), :] = total


def put(at, piece, first, mid, second):
    mid[at] = piece[C : 2 * C]
    first[at] = jnp.where(even("by"), piece[2 * C :], piece[:C])
    second[at] = jnp.where(even("by"), piece[:C], piece[2 * C :])


def back_own(
    table, fan_out, backward_z, ratio, first, out_mid, second, planes
):
    for view in range(V):
        back = dot(ratio[view].reshape(C * C, Z), backward_z[view])
        back = back.reshape(C, C, Z)
        taps = [table[view, t] for t in range(K)]
        for half in range(2):
            source = [back[i, 8 * half : 8 * half + 8, :] for i in range(C)]
            spread(source, taps, planes, view * C + 8 * half)

    for pair in range(N // 2):
        both = jnp.concatenate([planes[2 * pair], planes[2 * pair + 1]], axis=1)
        both = dot(
            fan_out[:, : 2 * V * C], jnp.concatenate(split(both), axis=0), None
        )
        both = both[:W] + both[W:]
        for part in range(2):
            piece = both[:, part * Z : (part + 1) * Z]
            put(2 * pair + part, piece, first, out_mid, second)


def back_rest(
    table, fan_pair, rest_z, far, near, after, out_first, out_mid, out_second, planes
):
    lane = lanes(8)
    front = lanes(W) < 64

    for pair in range(V // 2):
        block = [sides(near, far, 2 * pair + odd) for odd in range(2)]
        bands = [rest_z[2 * pair + odd] for odd in range(2)]
        back = dot(jnp.concatenate(block, axis=1), jnp.concatenate(bands, axis=0))
        back = back.reshape(C, C, Z)
        taps = [
            jnp.where(lane < 64, table[2 * pair, t], table[2 * pair + 1, t])
            for t in range(K)
        ]
        for half in range(2):
            rows = slice(8 * half, 8 * half + 8)
            source = [back[i, rows] for i in range(C)]
            spread(source, taps, planes, pair * C + 8 * half)

    planes[N] = jnp.zeros((W, Z), F32)
    planes[N + 1] = jnp.zeros((W, Z), F32)

    def fold(a):
        first, second = planes[a], planes[a + 1]
        turned, other = pltpu.roll(first, 64, 1), pltpu.roll(second, 64, 1)
        even_rows = jnp.where(front, first, other)
        odd_rows = jnp.where(front, turned, second)
        return jnp.concatenate([even_rows, odd_rows], axis=0)

    for quad in range(W // 4):
        both = jnp.concatenate([fold(4 * quad), fold(4 * quad + 2)], axis=1)
        both = dot(
            fan_pair[:, : 2 * V * C], jnp.concatenate(split(both), axis=0), None
        )
        both = both[:W] + both[W:]
        for part in range(min(2, N // 2 - 2 * quad)):
            piece = both[:, part * Z : (part + 1) * Z]
            put(2 * quad + part, piece, out_first, out_mid, out_second)


def add_rows(
    mid, from_low, from_high, rest, rest_low, rest_high, out_mid, first, second,
    out_low, out_high,
):
    lane = lanes(C)
    ends = jnp.logical_or(lane < 32, lane >= 96)
    out_low[0] = jnp.zeros((C, Z), F32)
    out_high[C - 1] = jnp.zeros((C, Z), F32)
    for a in range(N):
        below, above = choose("by", from_low[a], from_high[a])
        total = mid[a] + below + above
        below, above = choose("by", rest_low[a // 2], rest_high[a // 2])
        more = rest[a // 2] + below + above
        more = pltpu.roll(more, 32 if a % 2 else 96, 1)
        total = total + jnp.where(ends, more, 0.0)
        out = (out_low, out_mid, out_high)[(a + 1) // C]
        out[(a + 1) % C] = total
    first[...] = jnp.where(even("bx"), out_high[...], out_low[...])
    second[...] = jnp.where(even("bx"), out_low[...], out_high[...])


def part(tap, cell, count, which):
    before = jnp.where(tap > cell + R, 1.0, 0.0)
    after = jnp.where(tap < cell + R + 1 - count, 1.0, 0.0)
    return jnp.where(which == 0, before, jnp.where(which == 2, after, 1.0 - before - after))


def weigh(norm, estimate, marks, far_marks, near_marks, scale):
    has_low, has_high = edges("bz")
    tap = lax.broadcasted_iota(jnp.int32, (Z, Z), 0)
    cell = lax.broadcasted_iota(jnp.int32, (Z, Z), 1)
    part_x = [dot(norm[0], part(tap, cell, C, p), HIGHEST) for p in range(3)]
    part_z = [dot(norm[2], part(tap, cell, Z, r), HIGHEST) for r in range(3)]
    part_y = [dot(norm[1], part(tap, cell, C, q), HIGHEST) for q in range(3)]
    part_y = [jnp.concatenate([y] * C, axis=0).T for y in part_y]
    sums = [jnp.zeros((C, Z), F32) for _ in range(C)]
    for view in range(V):
        at = slice(view, view + 1)
        low = jnp.where(even(), far_marks[at], near_marks[at])
        high = jnp.where(even(), near_marks[at], far_marks[at])
        near = [
            jnp.where(has_low, low, 0.0),
            marks[at],
            jnp.where(has_high, high, 0.0),
        ]
        share = [
            jnp.broadcast_to(part_y[q][:C, view : view + 1], (C, Z)) for q in range(3)
        ]
        for p in range(3):
            term = None
            for r in range(3):
                level = None
                for q in range(3):
                    at = 3 * q + p
                    cell = jnp.broadcast_to(near[r][:, at : at + 1], (C, Z)) * share[q]
                    level = cell if level is None else level + cell
                level = level * part_z[r][view : view + 1, :]
                term = level if term is None else term + level
            for i in range(C):
                factor = jnp.broadcast_to(part_x[p][view : view + 1, i : i + 1], (C, Z))
                sums[i] = sums[i] + factor * term
    for i in range(C):
        scale[i] = estimate[i] / sums[i]


def finish(scale, mid, from_low, from_high, out):
    low, high = choose("bx", from_low[...], from_high[...])
    total = mid[...] + low + high
    out[...] = scale[...] * total


def on_device(estimate, raw, psf, offsets, coverage):
    cover = coverage.reshape(V)
    offsets = offsets.T
    full = (V, C, C, Z)

    left = trade(estimate, "bx", 0)
    right = trade(estimate, "bx", 1)
    up, down = call(
        pack_planes,
        [(V * OFF + 1, C, Z)] * 2,
        [HBM, VM],
        [pltpu.SMEM((V,), jnp.int32), pltpu.SemaphoreType.DMA],
        moved=3 << 19,
    )(cover, raw)
    raw_low = trade(up, "bx", 0)
    raw_high = trade(down, "bx", 1)
    (wide,) = call(
        join_planes,
        [(N, C, Z)],
        [HBM, VM, VM],
        [pltpu.SemaphoreType.DMA],
        moved=1 << 18,
    )(estimate, left, right)
    norm, table, fan_in, fan_out, fan_pair, forward_z, backward_z, rest_z = call(
        build,
        [
            (3, 8, Z),
            (V, K, 8, Z),
            jax.ShapeDtypeStruct((V * C, 2 * Z), BF16),
            jax.ShapeDtypeStruct((2 * W, 2 * Z), BF16),
            jax.ShapeDtypeStruct((2 * W, 2 * Z), BF16),
            (V, 2 * Z, Z),
            (V, Z, Z),
            (V, Z, Z),
        ],
        [SM, VM, ANY],
        moved=1 << 23,
    )(offsets, psf, wide)
    low = trade(wide, "by", 0)
    high = trade(wide, "by", 1)

    shifted, up, down, tiles = call(
        shift_planes,
        [
            (V, C, 2 * C, Z),
            (V * C + 1, OFF, Z),
            (V * C + 1, OFF, Z),
            (8, Z),
        ],
        [SM, SM, VM, VM, VM, ANY],
        [pltpu.VMEM((V, 2 * C, C, Z), F32)],
        moved=1 << 26,
    )(offsets, cover, raw, raw_low, raw_high, norm)
    raw_low = trade(up, "by", 0)
    raw_high = trade(down, "by", 1)

    blurred, near, far = call(
        forward,
        [full, (64 * V + 8, Z), (64 * V + 8, Z)],
        [VM] * 5 + [SM, ANY],
        [pltpu.VMEM((N, V * C, Z), F32)],
        flops=1 << 34,
        moved=1 << 26,
    )(table, fan_in, wide, low, high, cover, tiles)
    far, near = swap(far, 1), swap(near, 0)

    seen, marks, _ = call(
        shift_rows,
        [full, (8, Z), (V, C, 2 * C, Z)],
        [SM] + [VM] * 4 + [ANY],
        alias={1: 2},
        moved=1 << 26,
    )(offsets, shifted, raw_low, raw_high, tiles, blurred)

    (model,) = call(
        model_own, [full], [VM, VM, ANY], flops=1 << 30, moved=3 << 20
    )(forward_z, blurred, seen)
    ratio, near, far = call(
        divide,
        [full, (64 * V + 8, Z), (64 * V + 8, Z)],
        [SM, SM] + [VM] * 6,
        flops=1 << 34,
        moved=1 << 26,
    )(offsets, cover, forward_z, model, far, near, seen, marks)
    far, near = swap(far, 1), swap(near, 0)

    first, out_mid, second = call(
        back_own,
        [(N, C, Z)] * 3,
        [VM] * 4,
        [pltpu.VMEM((N, V * C, Z), F32)],
        flops=1 << 34,
        moved=1 << 26,
    )(table, fan_out, backward_z, ratio)
    sum_low = trade(first, "by", 0)
    sum_high = trade(second, "by", 1)
    rest_first, rest_mid, rest_second = call(
        back_rest,
        [(N // 2, C, Z)] * 3,
        [VM] * 5 + [ANY],
        [pltpu.VMEM((W, W, Z), F32)],
        flops=1 << 34,
        moved=1 << 26,
    )(table, fan_pair, rest_z, far, near, out_mid)
    more_low = trade(rest_first, "by", 0)
    more_high = trade(rest_second, "by", 1)
    last = pl.BlockSpec((8, Z), lambda i: (8 * V, 0))
    (scale,) = call(
        weigh, [(C, C, Z)], [VM, VM, VM, last, last], grid=(1,), moved=1 << 19
    )(norm, estimate, marks, far, near)
    out_mid, first, second = call(
        add_rows,
        [(C, C, Z)] * 3,
        [VM] * 6,
        [pltpu.VMEM((C, C, Z), F32)] * 2,
        moved=3 << 19,
    )(out_mid, sum_low, sum_high, rest_mid, more_low, more_high)
    sum_low = trade(first, "bx", 0)
    sum_high = trade(second, "bx", 1)
    (out,) = call(finish, [(C, C, Z)], [VM] * 4, moved=3 << 18)(
        scale, out_mid, sum_low, sum_high
    )
    return out


def solution(mesh):
    return jax.shard_map(
        on_device,
        mesh=mesh,
        in_specs=(
            P("bx", "by", "bz"),
            P(None, "bx", "by", "bz"),
            P(),
            P(),
            P(None, "bx", "by", "bz"),
        ),
        out_specs=P("bx", "by", "bz"),
        check_vma=False,
    )
```

```python
import jax
import jax.numpy as jnp
from jax import lax
from jax.experimental import pallas as pl
from jax.experimental.pallas import tpu as pltpu
from jax.sharding import PartitionSpec as P

V = 6
K = 31
R = 15
OFF = 8
C = 16
Z = 128
W = 3 * C
N = W - 2
HIGH = lax.Precision.HIGH
HIGHEST = lax.Precision.HIGHEST
F32 = jnp.float32
BF16 = jnp.bfloat16

VM = pl.BlockSpec(memory_space=pltpu.VMEM)
SM = pl.BlockSpec(memory_space=pltpu.SMEM)
ANY = pl.BlockSpec(memory_space=pl.ANY)
HBM = pl.BlockSpec(memory_space=pltpu.HBM)


def call(
    body, outs, specs, scratch=(), out_specs=None, grid=(), alias=None,
    flops=0, moved=0, vmem=16,
):
    return pl.pallas_call(
        body,
        grid=grid,
        out_shape=[
            s if hasattr(s, "dtype") else jax.ShapeDtypeStruct(s, F32) for s in outs
        ],
        in_specs=specs,
        out_specs=out_specs or [VM] * len(outs),
        scratch_shapes=list(scratch),
        input_output_aliases=alias or {},
        compiler_params=pltpu.CompilerParams(vmem_limit_bytes=vmem << 20),
        cost_estimate=pl.CostEstimate(
            flops=flops, bytes_accessed=moved, transcendentals=0
        ),
    )


def edges(axis):
    place = lax.axis_index(axis)
    return place > 0, place < lax.axis_size(axis) - 1


def even(axis="bz"):
    return lax.rem(lax.axis_index(axis), 2) == 0


def choose(axis, first, second):
    has_low, has_high = edges(axis)
    low = jnp.where(even(axis), second, first)
    high = jnp.where(even(axis), first, second)
    return jnp.where(has_low, low, 0.0), jnp.where(has_high, high, 0.0)


def trade(block, axis, first):
    count, depth = lax.axis_size(axis), lax.axis_size("bz")
    pairs = []
    for i in range(count):
        j = i + 1 if (i - first) % 2 == 0 else i - 1
        for z in range(depth):
            target = j * depth + z if 0 <= j < count else i * depth + (z ^ 1)
            pairs.append((i * depth + z, target))
    return lax.ppermute(block, (axis, "bz"), pairs)


def swap(block, first):
    count, depth = lax.axis_size("by"), lax.axis_size("bz")
    pairs = []
    for x in range(count):
        for z in range(depth):
            to = z + 1 if (z - first) % 2 == 0 else z - 1
            target = x * depth + to if 0 <= to < depth else (x ^ 1) * depth + z
            pairs.append((x * depth + z, target))
    return lax.ppermute(block, ("by", "bz"), pairs)


def lanes(rows):
    return lax.broadcasted_iota(jnp.int32, (rows, Z), 1)


def dot(a, b, precision=HIGH):
    return jnp.dot(a, b, precision=precision, preferred_element_type=F32)


def split(block):
    high = block.astype(BF16)
    return high, (block - high.astype(F32)).astype(BF16)


def pack_planes(cover, raw, up, down, flags, sem):
    tag = pltpu.make_async_copy(cover, flags, sem)
    tag.start()
    for view in range(V):
        at = slice(view * OFF, (view + 1) * OFF)
        up[at] = jnp.where(even("bx"), raw[view, OFF:], raw[view, :OFF])
        down[at] = jnp.where(even("bx"), raw[view, :OFF], raw[view, OFF:])
    tag.wait()
    for view in range(V):
        tile = jnp.full((1, Z), flags[view].astype(F32))
        up[V * OFF, view : view + 1] = tile
        down[V * OFF, view : view + 1] = tile


def build(
    offsets, psf, after, norm, table, fan_in, fan_out, fan_pair,
    forward_z, backward_z, rest_z,
):
    norm[...] = jnp.zeros((3, 8, Z), F32)
    for view in range(V):
        for axis in range(3):
            line = psf[view, axis : axis + 1, :]
            norm[axis, view : view + 1, 0:K] = line / jnp.sum(
                line, axis=1, keepdims=True
            )
    bands = []
    for view in range(V):
        line = norm[0, view : view + 1, :]
        for t in range(K):
            table[view, t] = jnp.broadcast_to(line[:, t : t + 1], (8, Z))
        row = jnp.broadcast_to(norm[1, view : view + 1, :], (C, Z))
        bands.append(pltpu.roll(row, 1, 1, stride=1, stride_axis=0))
        row = norm[2, view : view + 1, :]
        row = jnp.concatenate([row, jnp.zeros((1, Z), F32)], axis=1)
        row = jnp.broadcast_to(row, (2 * Z, 2 * Z))
        band = pltpu.roll(row, 2 * Z - R, 1, stride=1, stride_axis=0)
        band = pltpu.roll(band, lax.rem(2 * Z - offsets[2, view], 2 * Z), 1)
        backward_z[view] = band[:Z, :Z]
        rest_z[view] = pltpu.roll(band[Z:, :Z], 32 + 64 * (view % 2), 1)
        forward_z[view] = band[:Z, :].T
    def side_by_side(*parts):
        total = None
        for turn, block in parts:
            block = block.astype(F32)
            block = jnp.concatenate([block, jnp.zeros_like(block)], axis=1)
            block = pltpu.roll(block, turn, 1) if turn else block
            total = block if total is None else total + block
        return total.astype(BF16)

    high, low = split(jnp.concatenate(bands, axis=0))
    fan_in[...] = side_by_side((0, high), (W, high), (2 * W, low))
    for out, order in ((fan_out, range(V)), (fan_pair, (0, 2, 4, 1, 3, 5))):
        rows = [bands[v] for v in order]
        rows += [jnp.zeros((Z - V * C, Z), F32)]
        high, low = split(jnp.concatenate(rows, axis=0).T[:W, :])
        out[0:W] = side_by_side((0, high), (V * C, high))
        out[W:] = side_by_side((0, low), (V * C, low))


def join_planes(own, low, high, wide, sem):
    copy = pltpu.make_async_copy(own, wide.at[pl.ds(C - 1, C)], sem)
    copy.start()
    low, high = choose("bx", low[...], high[...])
    wide[: C - 1] = low[1:]
    wide[2 * C - 1 :] = high[: C - 1]
    copy.wait()


def pack_lanes(block, first):
    lane = lanes(64)
    packed = None
    for group in range(4):
        piece = block[4 * group : 4 * group + 4].reshape(64, Z)
        turn = (32 * group - first) % Z
        if turn:
            piece = pltpu.roll(piece, turn, 1)
        packed = piece if packed is None else jnp.where(lane >= 32 * group, piece, packed)
    return packed


def pack_sides(block, near, far, view):
    up = pack_lanes(block, 96)
    down = pack_lanes(block, 0)
    rows = pl.ds(pl.multiple_of(view * 64, 64), 64)
    near[rows, :] = jnp.where(even(), up, down)
    far[rows, :] = jnp.where(even(), down, up)


def forward(table, fan_in, own, low, high, cover, after, blurred, near, far, planes):
    fan = fan_in[:, : 3 * W]
    for pair in range(N // 2):
        sides = []
        for a in (2 * pair, 2 * pair + 1):
            below, above = choose("by", low[a], high[a])
            sides.append(jnp.concatenate([below, own[a], above], axis=0))
        top, rest = split(jnp.concatenate(sides, axis=1))
        both = dot(fan, jnp.concatenate([top, rest, top], axis=0), None)
        planes[2 * pair] = both[:, :Z]
        planes[2 * pair + 1] = both[:, Z:]

    for view in range(V):
        taps = [table[view, t] for t in range(K)]
        for half in range(2):
            sums = [None] * C
            for a in range(N):
                plane = planes[a, pl.ds(pl.multiple_of(view * C + 8 * half, 8), 8), :]
                for i in range(C):
                    t = a - i
                    if 0 <= t < K:
                        term = taps[t] * plane
                        sums[i] = term if sums[i] is None else sums[i] + term
            for i in range(C):
                blurred[view, i, 8 * half : 8 * half + 8, :] = sums[i]
        pack_sides(blurred[view], near, far, view)

    for view in range(V):
        tile = jnp.full((1, Z), cover[view].astype(F32))
        near[64 * V + view : 64 * V + view + 1] = tile
        far[64 * V + view : 64 * V + view + 1] = tile


def sides(near, far, view):
    has_low, has_high = edges("bz")
    lane = lanes(64)
    rows = pl.ds(pl.multiple_of(view * 64, 64), 64)
    near, far = near[rows, :], far[rows, :]
    low = jnp.where(even(), far, near)
    high = jnp.where(even(), near, far)
    parts = []
    for group in range(4):
        before = pltpu.roll(low, 96 - 32 * group, 1) if group < 3 else low
        after = pltpu.roll(high, (Z - 32 * group) % Z, 1) if group else high
        before = jnp.where(jnp.logical_and(lane >= 96, has_low), before, 0.0)
        after = jnp.where(jnp.logical_and(lane < 32, has_high), after, 0.0)
        parts.append(before + after)
    return jnp.concatenate(parts, axis=0)


def shift_planes(
    offsets, cover, raw, low, high, after, shifted, up, down, tiles, wide
):
    lane = lanes(8)
    row = lax.broadcasted_iota(jnp.int32, (8, Z), 0)
    own = jnp.zeros((8, Z), F32)
    for view in range(V):
        at = slice(view * OFF, (view + 1) * OFF)
        below, above = choose("bx", low[at], high[at])
        wide[view, 0:OFF] = below
        wide[view, OFF : OFF + C] = raw[view]
        wide[view, OFF + C :] = above
        block = wide[view, pl.ds(OFF + offsets[0, view], C)]
        shifted[view, :, OFF : OFF + C] = block
        at = slice(view * C, (view + 1) * C)
        up[at] = jnp.where(even("by"), block[:, OFF:], block[:, :OFF])
        down[at] = jnp.where(even("by"), block[:, :OFF], block[:, OFF:])
        own = jnp.where(row == view, cover[view].astype(F32), own)
    below, above = choose("bx", low[V * OFF, 0:8], high[V * OFF, 0:8])
    tile = jnp.where(lane == 0, below, jnp.where(lane == 1, own, above))
    tiles[...] = tile
    up[V * C] = tile
    down[V * C] = tile


def shift_rows(offsets, held, low, high, tiles, after, out, marks, main):
    lane = lanes(8)
    for view in range(V):
        at = slice(view * C, (view + 1) * C)
        below, above = choose("by", low[at], high[at])
        main[view, :, 0:OFF] = below
        main[view, :, OFF + C :] = above
        out[view] = main[view, :, pl.ds(OFF + offsets[1, view], C)]
    below, above = choose("by", low[V * C], high[V * C])
    middle = pltpu.roll(tiles[...], 3, 1)
    above = pltpu.roll(above, 6, 1)
    marks[...] = jnp.where(lane < 3, below, jnp.where(lane < 6, middle, above))


def model_own(forward_z, blurred, after, out):
    for view in range(V):
        block = dot(blurred[view].reshape(C * C, Z), forward_z[view, :Z])
        out[view] = block.reshape(C, C, Z)


def divide(
    offsets, cover, forward_z, model, high, low, seen, marks, ratio, near, far
):
    has_low, has_high = edges("bz")
    lane = lanes(1)
    for view in range(V):
        block = dot(sides(low, high, view), forward_z[view, Z:])
        block = model[view] + block.reshape(C, C, Z)
        at = slice(64 * V + view, 64 * V + view + 1)
        before = jnp.where(even(), high[at], low[at])
        after = jnp.where(even(), low[at], high[at])
        before = jnp.where(has_low, before, 0.0)
        after = jnp.where(has_high, after, 0.0)
        own = jnp.full((1, Z), cover[view].astype(F32))
        place = lane - offsets[2, view]
        mask = jnp.where(place < 0, before, jnp.where(place < Z, own, after))
        block = jnp.where(mask > 0.0, mask * seen[view] / block, 0.0)
        ratio[view] = block
        pack_sides(block, near, far, view)
    near[64 * V :] = marks[...]
    far[64 * V :] = marks[...]


def spread(source, taps, planes, row):
    for a in range(N):
        total = None
        for i in range(C):
            t = a - i
            if 0 <= t < K:
                term = taps[t] * source[i]
                total = term if total is None else total + term
        planes[a, pl.ds(pl.multiple_of(row, 8), 8), :] = total


def put(at, piece, first, mid, second):
    mid[at] = piece[C : 2 * C]
    first[at] = jnp.where(even("by"), piece[2 * C :], piece[:C])
    second[at] = jnp.where(even("by"), piece[:C], piece[2 * C :])


def back_own(
    table, fan_out, backward_z, ratio, first, out_mid, second, planes
):
    for view in range(V):
        back = dot(ratio[view].reshape(C * C, Z), backward_z[view])
        back = back.reshape(C, C, Z)
        taps = [table[view, t] for t in range(K)]
        for half in range(2):
            source = [back[i, 8 * half : 8 * half + 8, :] for i in range(C)]
            spread(source, taps, planes, view * C + 8 * half)

    for pair in range(N // 2):
        both = jnp.concatenate([planes[2 * pair], planes[2 * pair + 1]], axis=1)
        both = dot(
            fan_out[:, : 2 * V * C], jnp.concatenate(split(both), axis=0), None
        )
        both = both[:W] + both[W:]
        for part in range(2):
            piece = both[:, part * Z : (part + 1) * Z]
            put(2 * pair + part, piece, first, out_mid, second)


def back_rest(
    table, fan_pair, rest_z, far, near, after, out_first, out_mid, out_second, planes
):
    lane = lanes(8)
    front = lanes(W) < 64

    for pair in range(V // 2):
        block = [sides(near, far, 2 * pair + odd) for odd in range(2)]
        bands = [rest_z[2 * pair + odd] for odd in range(2)]
        back = dot(jnp.concatenate(block, axis=1), jnp.concatenate(bands, axis=0))
        back = back.reshape(C, C, Z)
        taps = [
            jnp.where(lane < 64, table[2 * pair, t], table[2 * pair + 1, t])
            for t in range(K)
        ]
        for half in range(2):
            rows = slice(8 * half, 8 * half + 8)
            source = [back[i, rows] for i in range(C)]
            spread(source, taps, planes, pair * C + 8 * half)

    planes[N] = jnp.zeros((W, Z), F32)
    planes[N + 1] = jnp.zeros((W, Z), F32)

    def fold(a):
        first, second = planes[a], planes[a + 1]
        turned, other = pltpu.roll(first, 64, 1), pltpu.roll(second, 64, 1)
        even_rows = jnp.where(front, first, other)
        odd_rows = jnp.where(front, turned, second)
        return jnp.concatenate([even_rows, odd_rows], axis=0)

    for quad in range(W // 4):
        both = jnp.concatenate([fold(4 * quad), fold(4 * quad + 2)], axis=1)
        both = dot(
            fan_pair[:, : 2 * V * C], jnp.concatenate(split(both), axis=0), None
        )
        both = both[:W] + both[W:]
        for part in range(min(2, N // 2 - 2 * quad)):
            piece = both[:, part * Z : (part + 1) * Z]
            put(2 * quad + part, piece, out_first, out_mid, out_second)


def add_own(mid, from_low, from_high, out_mid, first, second, out_low, out_high):
    out_low[0] = jnp.zeros((C, Z), F32)
    out_high[C - 1] = jnp.zeros((C, Z), F32)
    for a in range(N):
        below, above = choose("by", from_low[a], from_high[a])
        out = (out_low, out_mid, out_high)[(a + 1) // C]
        out[(a + 1) % C] = mid[a] + below + above
    first[...] = jnp.where(even("bx"), out_high[...], out_low[...])
    second[...] = jnp.where(even("bx"), out_low[...], out_high[...])


def add_rest(rest, from_low, from_high, after, mid, first, second):
    below, above = choose("by", from_low[...], from_high[...])
    total = rest[...] + below + above
    low, high = total[:8], total[15:]
    mid[...] = total[7:16]
    first[...] = jnp.where(even("bx"), high, low)
    second[...] = jnp.where(even("bx"), low, high)


def part(tap, cell, count, which):
    before = jnp.where(tap > cell + R, 1.0, 0.0)
    after = jnp.where(tap < cell + R + 1 - count, 1.0, 0.0)
    return jnp.where(which == 0, before, jnp.where(which == 2, after, 1.0 - before - after))


def weigh(norm, estimate, marks, far_marks, near_marks, scale):
    has_low, has_high = edges("bz")
    tap = lax.broadcasted_iota(jnp.int32, (Z, Z), 0)
    cell = lax.broadcasted_iota(jnp.int32, (Z, Z), 1)
    part_x = [dot(norm[0], part(tap, cell, C, p), HIGHEST) for p in range(3)]
    part_z = [dot(norm[2], part(tap, cell, Z, r), HIGHEST) for r in range(3)]
    part_y = [dot(norm[1], part(tap, cell, C, q), HIGHEST) for q in range(3)]
    part_y = [jnp.concatenate([y] * C, axis=0).T for y in part_y]
    sums = [jnp.zeros((C, Z), F32) for _ in range(C)]
    for view in range(V):
        at = slice(view, view + 1)
        low = jnp.where(even(), far_marks[at], near_marks[at])
        high = jnp.where(even(), near_marks[at], far_marks[at])
        near = [
            jnp.where(has_low, low, 0.0),
            marks[at],
            jnp.where(has_high, high, 0.0),
        ]
        share = [
            jnp.broadcast_to(part_y[q][:C, view : view + 1], (C, Z)) for q in range(3)
        ]
        for p in range(3):
            term = None
            for r in range(3):
                level = None
                for q in range(3):
                    at = 3 * q + p
                    cell = jnp.broadcast_to(near[r][:, at : at + 1], (C, Z)) * share[q]
                    level = cell if level is None else level + cell
                level = level * part_z[r][view : view + 1, :]
                term = level if term is None else term + level
            for i in range(C):
                factor = jnp.broadcast_to(part_x[p][view : view + 1, i : i + 1], (C, Z))
                sums[i] = sums[i] + factor * term
    for i in range(C):
        scale[i] = estimate[i] / sums[i]


def finish(scale, mid, from_low, from_high, rest, rest_low, rest_high, out):
    low, high = choose("bx", from_low[...], from_high[...])
    below, above = choose("bx", rest_low[...], rest_high[...])
    lane = lanes(C)
    ends = jnp.logical_or(lane < 32, lane >= 96)
    for x in range(C):
        n, second = (C - 1 + x) // 2 - 7, (C - 1 + x) % 2
        more = rest[n]
        if n < 8:
            more = more + below[n]
        if n > 0:
            more = more + above[n - 1]
        more = jnp.where(ends, pltpu.roll(more, 32 if second else 96, 1), 0.0)
        out[x] = scale[x] * (mid[x] + low[x] + high[x] + more)


def on_device(estimate, raw, psf, offsets, coverage):
    cover = coverage.reshape(V)
    offsets = offsets.T
    full = (V, C, C, Z)

    left = trade(estimate, "bx", 0)
    right = trade(estimate, "bx", 1)
    up, down = call(
        pack_planes,
        [(V * OFF + 1, C, Z)] * 2,
        [HBM, VM],
        [pltpu.SMEM((V,), jnp.int32), pltpu.SemaphoreType.DMA],
        moved=3 << 19,
    )(cover, raw)
    raw_low = trade(up, "bx", 0)
    raw_high = trade(down, "bx", 1)
    (wide,) = call(
        join_planes,
        [(N, C, Z)],
        [HBM, VM, VM],
        [pltpu.SemaphoreType.DMA],
        moved=1 << 18,
    )(estimate, left, right)
    norm, table, fan_in, fan_out, fan_pair, forward_z, backward_z, rest_z = call(
        build,
        [
            (3, 8, Z),
            (V, K, 8, Z),
            jax.ShapeDtypeStruct((V * C, 2 * Z), BF16),
            jax.ShapeDtypeStruct((2 * W, 2 * Z), BF16),
            jax.ShapeDtypeStruct((2 * W, 2 * Z), BF16),
            (V, 2 * Z, Z),
            (V, Z, Z),
            (V, Z, Z),
        ],
        [SM, VM, ANY],
        moved=1 << 23,
    )(offsets, psf, wide)
    low = trade(wide, "by", 0)
    high = trade(wide, "by", 1)

    shifted, up, down, tiles = call(
        shift_planes,
        [
            (V, C, 2 * C, Z),
            (V * C + 1, OFF, Z),
            (V * C + 1, OFF, Z),
            (8, Z),
        ],
        [SM, SM, VM, VM, VM, ANY],
        [pltpu.VMEM((V, 2 * C, C, Z), F32)],
        moved=1 << 26,
    )(offsets, cover, raw, raw_low, raw_high, norm)
    raw_low = trade(up, "by", 0)
    raw_high = trade(down, "by", 1)

    blurred, near, far = call(
        forward,
        [full, (64 * V + 8, Z), (64 * V + 8, Z)],
        [VM] * 5 + [SM, ANY],
        [pltpu.VMEM((N, V * C, Z), F32)],
        flops=1 << 34,
        moved=1 << 26,
    )(table, fan_in, wide, low, high, cover, tiles)
    far, near = swap(far, 1), swap(near, 0)

    seen, marks, _ = call(
        shift_rows,
        [full, (8, Z), (V, C, 2 * C, Z)],
        [SM] + [VM] * 4 + [ANY],
        alias={1: 2},
        moved=1 << 26,
    )(offsets, shifted, raw_low, raw_high, tiles, blurred)

    (model,) = call(
        model_own, [full], [VM, VM, ANY], flops=1 << 30, moved=3 << 20
    )(forward_z, blurred, seen)
    ratio, near, far = call(
        divide,
        [full, (64 * V + 8, Z), (64 * V + 8, Z)],
        [SM, SM] + [VM] * 6,
        flops=1 << 34,
        moved=1 << 26,
    )(offsets, cover, forward_z, model, far, near, seen, marks)
    far, near = swap(far, 1), swap(near, 0)

    first, out_mid, second = call(
        back_own,
        [(N, C, Z)] * 3,
        [VM] * 4,
        [pltpu.VMEM((N, V * C, Z), F32)],
        flops=1 << 34,
        moved=1 << 26,
    )(table, fan_out, backward_z, ratio)
    sum_low = trade(first, "by", 0)
    sum_high = trade(second, "by", 1)
    rest_first, rest_mid, rest_second = call(
        back_rest,
        [(N // 2, C, Z)] * 3,
        [VM] * 5 + [ANY],
        [pltpu.VMEM((W, W, Z), F32)],
        flops=1 << 34,
        moved=1 << 26,
    )(table, fan_pair, rest_z, far, near, out_mid)
    more_low = trade(rest_first, "by", 0)
    more_high = trade(rest_second, "by", 1)
    out_mid, first, second = call(
        add_own,
        [(C, C, Z)] * 3,
        [VM] * 3,
        [pltpu.VMEM((C, C, Z), F32)] * 2,
        moved=3 << 19,
    )(out_mid, sum_low, sum_high)
    sum_low = trade(first, "bx", 0)
    sum_high = trade(second, "bx", 1)
    rest_mid, first, second = call(
        add_rest,
        [(9, C, Z), (8, C, Z), (8, C, Z)],
        [VM] * 3 + [ANY],
        flops=1 << 34,
        moved=1 << 26,
    )(rest_mid, more_low, more_high, out_mid)
    more_low = trade(first, "bx", 0)
    more_high = trade(second, "bx", 1)
    last = pl.BlockSpec((8, Z), lambda i: (8 * V, 0))
    (scale,) = call(
        weigh, [(C, C, Z)], [VM, VM, VM, last, last], grid=(1,), moved=1 << 19
    )(norm, estimate, marks, far, near)
    (out,) = call(finish, [(C, C, Z)], [VM] * 7, moved=3 << 18)(
        scale, out_mid, sum_low, sum_high, rest_mid, more_low, more_high
    )
    return out


def solution(mesh):
    return jax.shard_map(
        on_device,
        mesh=mesh,
        in_specs=(
            P("bx", "by", "bz"),
            P(None, "bx", "by", "bz"),
            P(),
            P(),
            P(None, "bx", "by", "bz"),
        ),
        out_specs=P("bx", "by", "bz"),
        check_vma=False,
    )
```

```python
import jax
import jax.numpy as jnp
from jax import lax
from jax.experimental import pallas as pl
from jax.experimental.pallas import tpu as pltpu
from jax.sharding import PartitionSpec as P

V = 6
K = 31
R = 15
OFF = 8
C = 16
Z = 128
W = 3 * C
N = W - 2
HIGH = lax.Precision.HIGH
HIGHEST = lax.Precision.HIGHEST
F32 = jnp.float32
BF16 = jnp.bfloat16

VM = pl.BlockSpec(memory_space=pltpu.VMEM)
SM = pl.BlockSpec(memory_space=pltpu.SMEM)
ANY = pl.BlockSpec(memory_space=pl.ANY)
HBM = pl.BlockSpec(memory_space=pltpu.HBM)


def call(
    body, outs, specs, scratch=(), out_specs=None, grid=(), alias=None,
    flops=0, moved=0, vmem=16,
):
    return pl.pallas_call(
        body,
        grid=grid,
        out_shape=[
            s if hasattr(s, "dtype") else jax.ShapeDtypeStruct(s, F32) for s in outs
        ],
        in_specs=specs,
        out_specs=out_specs or [VM] * len(outs),
        scratch_shapes=list(scratch),
        input_output_aliases=alias or {},
        compiler_params=pltpu.CompilerParams(vmem_limit_bytes=vmem << 20),
        cost_estimate=pl.CostEstimate(
            flops=flops, bytes_accessed=moved, transcendentals=0
        ),
    )


def edges(axis):
    place = lax.axis_index(axis)
    return place > 0, place < lax.axis_size(axis) - 1


def even(axis="bz"):
    return lax.rem(lax.axis_index(axis), 2) == 0


def choose(axis, first, second):
    has_low, has_high = edges(axis)
    low = jnp.where(even(axis), second, first)
    high = jnp.where(even(axis), first, second)
    return jnp.where(has_low, low, 0.0), jnp.where(has_high, high, 0.0)


def trade(block, axis, first):
    count, depth = lax.axis_size(axis), lax.axis_size("bz")
    pairs = []
    for i in range(count):
        j = i + 1 if (i - first) % 2 == 0 else i - 1
        for z in range(depth):
            target = j * depth + z if 0 <= j < count else i * depth + (z ^ 1)
            pairs.append((i * depth + z, target))
    return lax.ppermute(block, (axis, "bz"), pairs)


def swap(block, first):
    count, depth = lax.axis_size("bx"), lax.axis_size("bz")
    pairs = []
    for x in range(count):
        for z in range(depth):
            to = z + 1 if (z - first) % 2 == 0 else z - 1
            target = x * depth + to if 0 <= to < depth else (x ^ 1) * depth + z
            pairs.append((x * depth + z, target))
    return lax.ppermute(block, ("bx", "bz"), pairs)


def lanes(rows):
    return lax.broadcasted_iota(jnp.int32, (rows, Z), 1)


def dot(a, b, precision=HIGH):
    return jnp.dot(a, b, precision=precision, preferred_element_type=F32)


def split(block):
    high = block.astype(BF16)
    return high, (block - high.astype(F32)).astype(BF16)


def pack_planes(cover, raw, up, down, flags, sem):
    tag = pltpu.make_async_copy(cover, flags, sem)
    tag.start()
    for view in range(V):
        at = slice(view * OFF, (view + 1) * OFF)
        up[at] = jnp.where(even("bx"), raw[view, OFF:], raw[view, :OFF])
        down[at] = jnp.where(even("bx"), raw[view, :OFF], raw[view, OFF:])
    tag.wait()
    for view in range(V):
        tile = jnp.full((1, Z), flags[view].astype(F32))
        up[V * OFF, view : view + 1] = tile
        down[V * OFF, view : view + 1] = tile


def build(
    offsets, psf, after, norm, table, fan_in, fan_out, fan_pair,
    forward_z, backward_z, rest_z,
):
    norm[...] = jnp.zeros((3, 8, Z), F32)
    for view in range(V):
        for axis in range(3):
            line = psf[view, axis : axis + 1, :]
            norm[axis, view : view + 1, 0:K] = line / jnp.sum(
                line, axis=1, keepdims=True
            )
    bands = []
    for view in range(V):
        line = norm[0, view : view + 1, :]
        for t in range(K):
            table[view, t] = jnp.broadcast_to(line[:, t : t + 1], (8, Z))
        row = jnp.broadcast_to(norm[1, view : view + 1, :], (C, Z))
        bands.append(pltpu.roll(row, 1, 1, stride=1, stride_axis=0))
        row = norm[2, view : view + 1, :]
        row = jnp.concatenate([row, jnp.zeros((1, Z), F32)], axis=1)
        row = jnp.broadcast_to(row, (2 * Z, 2 * Z))
        band = pltpu.roll(row, 2 * Z - R, 1, stride=1, stride_axis=0)
        band = pltpu.roll(band, lax.rem(2 * Z - offsets[2, view], 2 * Z), 1)
        backward_z[view] = band[:Z, :Z]
        rest_z[view] = pltpu.roll(band[Z:, :Z], 32 + 64 * (view % 2), 1)
        forward_z[view] = band[:Z, :].T
    def side_by_side(*parts):
        total = None
        for turn, block in parts:
            block = block.astype(F32)
            block = jnp.concatenate([block, jnp.zeros_like(block)], axis=1)
            block = pltpu.roll(block, turn, 1) if turn else block
            total = block if total is None else total + block
        return total.astype(BF16)

    high, low = split(jnp.concatenate(bands, axis=0))
    fan_in[...] = side_by_side((0, high), (W, high), (2 * W, low))
    for out, order in ((fan_out, range(V)), (fan_pair, (0, 2, 4, 1, 3, 5))):
        rows = [bands[v] for v in order]
        rows += [jnp.zeros((Z - V * C, Z), F32)]
        high, low = split(jnp.concatenate(rows, axis=0).T[:W, :])
        out[0:W] = side_by_side((0, high), (V * C, high))
        out[W:] = side_by_side((0, low), (V * C, low))


def join_planes(own, low, high, wide, sem):
    copy = pltpu.make_async_copy(own, wide.at[pl.ds(C - 1, C)], sem)
    copy.start()
    low, high = choose("bx", low[...], high[...])
    wide[: C - 1] = low[1:]
    wide[2 * C - 1 :] = high[: C - 1]
    copy.wait()


def pack_lanes(block, first):
    lane = lanes(64)
    packed = None
    for group in range(4):
        piece = block[4 * group : 4 * group + 4].reshape(64, Z)
        turn = (32 * group - first) % Z
        if turn:
            piece = pltpu.roll(piece, turn, 1)
        packed = piece if packed is None else jnp.where(lane >= 32 * group, piece, packed)
    return packed


def pack_sides(block, near, far, view):
    up = pack_lanes(block, 96)
    down = pack_lanes(block, 0)
    rows = pl.ds(pl.multiple_of(view * 64, 64), 64)
    near[rows, :] = jnp.where(even(), up, down)
    far[rows, :] = jnp.where(even(), down, up)


def forward(table, fan_in, own, low, high, cover, after, blurred, near, far, planes):
    fan = fan_in[:, : 3 * W]
    for pair in range(N // 2):
        sides = []
        for a in (2 * pair, 2 * pair + 1):
            below, above = choose("by", low[a], high[a])
            sides.append(jnp.concatenate([below, own[a], above], axis=0))
        top, rest = split(jnp.concatenate(sides, axis=1))
        both = dot(fan, jnp.concatenate([top, rest, top], axis=0), None)
        planes[2 * pair] = both[:, :Z]
        planes[2 * pair + 1] = both[:, Z:]

    for view in range(V):
        taps = [table[view, t] for t in range(K)]
        for half in range(2):
            sums = [None] * C
            for a in range(N):
                plane = planes[a, pl.ds(pl.multiple_of(view * C + 8 * half, 8), 8), :]
                for i in range(C):
                    t = a - i
                    if 0 <= t < K:
                        term = taps[t] * plane
                        sums[i] = term if sums[i] is None else sums[i] + term
            for i in range(C):
                blurred[view, i, 8 * half : 8 * half + 8, :] = sums[i]
        pack_sides(blurred[view], near, far, view)

    for view in range(V):
        tile = jnp.full((1, Z), cover[view].astype(F32))
        near[64 * V + view : 64 * V + view + 1] = tile
        far[64 * V + view : 64 * V + view + 1] = tile


def sides(near, far, view):
    has_low, has_high = edges("bz")
    lane = lanes(64)
    rows = pl.ds(pl.multiple_of(view * 64, 64), 64)
    near, far = near[rows, :], far[rows, :]
    low = jnp.where(even(), far, near)
    high = jnp.where(even(), near, far)
    parts = []
    for group in range(4):
        before = pltpu.roll(low, 96 - 32 * group, 1) if group < 3 else low
        after = pltpu.roll(high, (Z - 32 * group) % Z, 1) if group else high
        before = jnp.where(jnp.logical_and(lane >= 96, has_low), before, 0.0)
        after = jnp.where(jnp.logical_and(lane < 32, has_high), after, 0.0)
        parts.append(before + after)
    return jnp.concatenate(parts, axis=0)


def shift_planes(
    offsets, cover, raw, low, high, after, shifted, up, down, tiles, wide
):
    lane = lanes(8)
    row = lax.broadcasted_iota(jnp.int32, (8, Z), 0)
    own = jnp.zeros((8, Z), F32)
    for view in range(V):
        at = slice(view * OFF, (view + 1) * OFF)
        below, above = choose("bx", low[at], high[at])
        wide[view, 0:OFF] = below
        wide[view, OFF : OFF + C] = raw[view]
        wide[view, OFF + C :] = above
        block = wide[view, pl.ds(OFF + offsets[0, view], C)]
        shifted[view, :, OFF : OFF + C] = block
        at = slice(view * C, (view + 1) * C)
        up[at] = jnp.where(even("by"), block[:, OFF:], block[:, :OFF])
        down[at] = jnp.where(even("by"), block[:, :OFF], block[:, OFF:])
        own = jnp.where(row == view, cover[view].astype(F32), own)
    below, above = choose("bx", low[V * OFF, 0:8], high[V * OFF, 0:8])
    tile = jnp.where(lane == 0, below, jnp.where(lane == 1, own, above))
    tiles[...] = tile
    up[V * C] = tile
    down[V * C] = tile


def shift_rows(offsets, held, low, high, tiles, after, out, marks, main):
    lane = lanes(8)
    for view in range(V):
        at = slice(view * C, (view + 1) * C)
        below, above = choose("by", low[at], high[at])
        main[view, :, 0:OFF] = below
        main[view, :, OFF + C :] = above
        out[view] = main[view, :, pl.ds(OFF + offsets[1, view], C)]
    below, above = choose("by", low[V * C], high[V * C])
    middle = pltpu.roll(tiles[...], 3, 1)
    above = pltpu.roll(above, 6, 1)
    marks[...] = jnp.where(lane < 3, below, jnp.where(lane < 6, middle, above))


def model_own(forward_z, blurred, after, out):
    for view in range(V):
        block = dot(blurred[view].reshape(C * C, Z), forward_z[view, :Z])
        out[view] = block.reshape(C, C, Z)


def divide(
    offsets, cover, forward_z, model, high, low, seen, marks, ratio, near, far
):
    has_low, has_high = edges("bz")
    lane = lanes(1)
    for view in range(V):
        block = dot(sides(low, high, view), forward_z[view, Z:])
        block = model[view] + block.reshape(C, C, Z)
        at = slice(64 * V + view, 64 * V + view + 1)
        before = jnp.where(even(), high[at], low[at])
        after = jnp.where(even(), low[at], high[at])
        before = jnp.where(has_low, before, 0.0)
        after = jnp.where(has_high, after, 0.0)
        own = jnp.full((1, Z), cover[view].astype(F32))
        place = lane - offsets[2, view]
        mask = jnp.where(place < 0, before, jnp.where(place < Z, own, after))
        block = jnp.where(mask > 0.0, mask * seen[view] / block, 0.0)
        ratio[view] = block
        pack_sides(block, near, far, view)
    near[64 * V :] = marks[...]
    far[64 * V :] = marks[...]


def spread(source, taps, planes, row):
    for a in range(N):
        total = None
        for i in range(C):
            t = a - i
            if 0 <= t < K:
                term = taps[t] * source[i]
                total = term if total is None else total + term
        planes[a, pl.ds(pl.multiple_of(row, 8), 8), :] = total


def put(at, piece, first, mid, second):
    mid[at] = piece[C : 2 * C]
    first[at] = jnp.where(even("by"), piece[2 * C :], piece[:C])
    second[at] = jnp.where(even("by"), piece[:C], piece[2 * C :])


def back_own(
    table, fan_out, backward_z, ratio, first, out_mid, second, planes
):
    for view in range(V):
        back = dot(ratio[view].reshape(C * C, Z), backward_z[view])
        back = back.reshape(C, C, Z)
        taps = [table[view, t] for t in range(K)]
        for half in range(2):
            source = [back[i, 8 * half : 8 * half + 8, :] for i in range(C)]
            spread(source, taps, planes, view * C + 8 * half)

    for pair in range(N // 2):
        both = jnp.concatenate([planes[2 * pair], planes[2 * pair + 1]], axis=1)
        both = dot(
            fan_out[:, : 2 * V * C], jnp.concatenate(split(both), axis=0), None
        )
        both = both[:W] + both[W:]
        for part in range(2):
            piece = both[:, part * Z : (part + 1) * Z]
            put(2 * pair + part, piece, first, out_mid, second)


def back_rest(
    table, fan_pair, rest_z, far, near, after, out_first, out_mid, out_second, planes
):
    lane = lanes(8)
    front = lanes(W) < 64

    for pair in range(V // 2):
        block = [sides(near, far, 2 * pair + odd) for odd in range(2)]
        bands = [rest_z[2 * pair + odd] for odd in range(2)]
        back = dot(jnp.concatenate(block, axis=1), jnp.concatenate(bands, axis=0))
        back = back.reshape(C, C, Z)
        taps = [
            jnp.where(lane < 64, table[2 * pair, t], table[2 * pair + 1, t])
            for t in range(K)
        ]
        for half in range(2):
            rows = slice(8 * half, 8 * half + 8)
            source = [back[i, rows] for i in range(C)]
            spread(source, taps, planes, pair * C + 8 * half)

    planes[N] = jnp.zeros((W, Z), F32)
    planes[N + 1] = jnp.zeros((W, Z), F32)

    def fold(a):
        first, second = planes[a], planes[a + 1]
        turned, other = pltpu.roll(first, 64, 1), pltpu.roll(second, 64, 1)
        even_rows = jnp.where(front, first, other)
        odd_rows = jnp.where(front, turned, second)
        return jnp.concatenate([even_rows, odd_rows], axis=0)

    for quad in range(W // 4):
        both = jnp.concatenate([fold(4 * quad), fold(4 * quad + 2)], axis=1)
        both = dot(
            fan_pair[:, : 2 * V * C], jnp.concatenate(split(both), axis=0), None
        )
        both = both[:W] + both[W:]
        for part in range(min(2, N // 2 - 2 * quad)):
            piece = both[:, part * Z : (part + 1) * Z]
            put(2 * quad + part, piece, out_first, out_mid, out_second)


def add_own(mid, from_low, from_high, out_mid, first, second, out_low, out_high):
    out_low[0] = jnp.zeros((C, Z), F32)
    out_high[C - 1] = jnp.zeros((C, Z), F32)
    for a in range(N):
        below, above = choose("by", from_low[a], from_high[a])
        out = (out_low, out_mid, out_high)[(a + 1) // C]
        out[(a + 1) % C] = mid[a] + below + above
    first[...] = jnp.where(even("bx"), out_high[...], out_low[...])
    second[...] = jnp.where(even("bx"), out_low[...], out_high[...])


def add_rest(rest, from_low, from_high, after, mid, first, second):
    below, above = choose("by", from_low[...], from_high[...])
    total = rest[...] + below + above
    low, high = total[:8], total[15:]
    mid[...] = total[7:16]
    first[...] = jnp.where(even("bx"), high, low)
    second[...] = jnp.where(even("bx"), low, high)


def part(tap, cell, count, which):
    before = jnp.where(tap > cell + R, 1.0, 0.0)
    after = jnp.where(tap < cell + R + 1 - count, 1.0, 0.0)
    return jnp.where(which == 0, before, jnp.where(which == 2, after, 1.0 - before - after))


def weigh(norm, estimate, marks, far_marks, near_marks, scale):
    has_low, has_high = edges("bz")
    tap = lax.broadcasted_iota(jnp.int32, (Z, Z), 0)
    cell = lax.broadcasted_iota(jnp.int32, (Z, Z), 1)
    part_x = [dot(norm[0], part(tap, cell, C, p), HIGHEST) for p in range(3)]
    part_z = [dot(norm[2], part(tap, cell, Z, r), HIGHEST) for r in range(3)]
    part_y = [dot(norm[1], part(tap, cell, C, q), HIGHEST) for q in range(3)]
    part_y = [jnp.concatenate([y] * C, axis=0).T for y in part_y]
    sums = [jnp.zeros((C, Z), F32) for _ in range(C)]
    for view in range(V):
        at = slice(view, view + 1)
        low = jnp.where(even(), far_marks[at], near_marks[at])
        high = jnp.where(even(), near_marks[at], far_marks[at])
        near = [
            jnp.where(has_low, low, 0.0),
            marks[at],
            jnp.where(has_high, high, 0.0),
        ]
        share = [
            jnp.broadcast_to(part_y[q][:C, view : view + 1], (C, Z)) for q in range(3)
        ]
        for p in range(3):
            term = None
            for r in range(3):
                level = None
                for q in range(3):
                    at = 3 * q + p
                    cell = jnp.broadcast_to(near[r][:, at : at + 1], (C, Z)) * share[q]
                    level = cell if level is None else level + cell
                level = level * part_z[r][view : view + 1, :]
                term = level if term is None else term + level
            for i in range(C):
                factor = jnp.broadcast_to(part_x[p][view : view + 1, i : i + 1], (C, Z))
                sums[i] = sums[i] + factor * term
    for i in range(C):
        scale[i] = estimate[i] / sums[i]


def finish(scale, mid, from_low, from_high, rest, rest_low, rest_high, out):
    low, high = choose("bx", from_low[...], from_high[...])
    below, above = choose("bx", rest_low[...], rest_high[...])
    lane = lanes(C)
    ends = jnp.logical_or(lane < 32, lane >= 96)
    for x in range(C):
        n, second = (C - 1 + x) // 2 - 7, (C - 1 + x) % 2
        more = rest[n]
        if n < 8:
            more = more + below[n]
        if n > 0:
            more = more + above[n - 1]
        more = jnp.where(ends, pltpu.roll(more, 32 if second else 96, 1), 0.0)
        out[x] = scale[x] * (mid[x] + low[x] + high[x] + more)


def on_device(estimate, raw, psf, offsets, coverage):
    cover = coverage.reshape(V)
    offsets = offsets.T
    full = (V, C, C, Z)

    left = trade(estimate, "bx", 0)
    right = trade(estimate, "bx", 1)
    up, down = call(
        pack_planes,
        [(V * OFF + 1, C, Z)] * 2,
        [HBM, VM],
        [pltpu.SMEM((V,), jnp.int32), pltpu.SemaphoreType.DMA],
        moved=3 << 19,
    )(cover, raw)
    raw_low = trade(up, "bx", 0)
    raw_high = trade(down, "bx", 1)
    (wide,) = call(
        join_planes,
        [(N, C, Z)],
        [HBM, VM, VM],
        [pltpu.SemaphoreType.DMA],
        moved=1 << 18,
    )(estimate, left, right)
    norm, table, fan_in, fan_out, fan_pair, forward_z, backward_z, rest_z = call(
        build,
        [
            (3, 8, Z),
            (V, K, 8, Z),
            jax.ShapeDtypeStruct((V * C, 2 * Z), BF16),
            jax.ShapeDtypeStruct((2 * W, 2 * Z), BF16),
            jax.ShapeDtypeStruct((2 * W, 2 * Z), BF16),
            (V, 2 * Z, Z),
            (V, Z, Z),
            (V, Z, Z),
        ],
        [SM, VM, ANY],
        moved=1 << 23,
    )(offsets, psf, wide)
    low = trade(wide, "by", 0)
    high = trade(wide, "by", 1)

    shifted, up, down, tiles = call(
        shift_planes,
        [
            (V, C, 2 * C, Z),
            (V * C + 1, OFF, Z),
            (V * C + 1, OFF, Z),
            (8, Z),
        ],
        [SM, SM, VM, VM, VM, ANY],
        [pltpu.VMEM((V, 2 * C, C, Z), F32)],
        moved=1 << 26,
    )(offsets, cover, raw, raw_low, raw_high, norm)
    raw_low = trade(up, "by", 0)
    raw_high = trade(down, "by", 1)

    blurred, near, far = call(
        forward,
        [full, (64 * V + 8, Z), (64 * V + 8, Z)],
        [VM] * 5 + [SM, ANY],
        [pltpu.VMEM((N, V * C, Z), F32)],
        flops=1 << 34,
        moved=1 << 26,
    )(table, fan_in, wide, low, high, cover, tiles)
    far, near = swap(far, 1), swap(near, 0)

    seen, marks, _ = call(
        shift_rows,
        [full, (8, Z), (V, C, 2 * C, Z)],
        [SM] + [VM] * 4 + [ANY],
        alias={1: 2},
        moved=1 << 26,
    )(offsets, shifted, raw_low, raw_high, tiles, blurred)

    (model,) = call(
        model_own, [full], [VM, VM, ANY], flops=1 << 30, moved=3 << 20
    )(forward_z, blurred, seen)
    ratio, near, far = call(
        divide,
        [full, (64 * V + 8, Z), (64 * V + 8, Z)],
        [SM, SM] + [VM] * 6,
        flops=1 << 34,
        moved=1 << 26,
    )(offsets, cover, forward_z, model, far, near, seen, marks)
    far, near = swap(far, 1), swap(near, 0)

    first, out_mid, second = call(
        back_own,
        [(N, C, Z)] * 3,
        [VM] * 4,
        [pltpu.VMEM((N, V * C, Z), F32)],
        flops=1 << 34,
        moved=1 << 26,
    )(table, fan_out, backward_z, ratio)
    sum_low = trade(first, "by", 0)
    sum_high = trade(second, "by", 1)
    rest_first, rest_mid, rest_second = call(
        back_rest,
        [(N // 2, C, Z)] * 3,
        [VM] * 5 + [ANY],
        [pltpu.VMEM((W, W, Z), F32)],
        flops=1 << 34,
        moved=1 << 26,
    )(table, fan_pair, rest_z, far, near, out_mid)
    more_low = trade(rest_first, "by", 0)
    more_high = trade(rest_second, "by", 1)
    out_mid, first, second = call(
        add_own,
        [(C, C, Z)] * 3,
        [VM] * 3,
        [pltpu.VMEM((C, C, Z), F32)] * 2,
        moved=3 << 19,
    )(out_mid, sum_low, sum_high)
    sum_low = trade(first, "bx", 0)
    sum_high = trade(second, "bx", 1)
    rest_mid, first, second = call(
        add_rest,
        [(9, C, Z), (8, C, Z), (8, C, Z)],
        [VM] * 3 + [ANY],
        flops=1 << 34,
        moved=1 << 26,
    )(rest_mid, more_low, more_high, out_mid)
    more_low = trade(first, "bx", 0)
    more_high = trade(second, "bx", 1)
    last = pl.BlockSpec((8, Z), lambda i: (8 * V, 0))
    (scale,) = call(
        weigh, [(C, C, Z)], [VM, VM, VM, last, last], grid=(1,), moved=1 << 19
    )(norm, estimate, marks, far, near)
    (out,) = call(finish, [(C, C, Z)], [VM] * 7, moved=3 << 18)(
        scale, out_mid, sum_low, sum_high, rest_mid, more_low, more_high
    )
    return out


def solution(mesh):
    return jax.shard_map(
        on_device,
        mesh=mesh,
        in_specs=(
            P("bx", "by", "bz"),
            P(None, "bx", "by", "bz"),
            P(),
            P(),
            P(None, "bx", "by", "bz"),
        ),
        out_specs=P("bx", "by", "bz"),
        check_vma=False,
    )
```
